256 devices in a mesh: wl: 8 (over y, z_lo), gz: 32 (over z_hi, x, core).
Axes of the slice: x: 4, y: 4, z: 8 (z_hi: 4, z_lo: 2; z = z_hi * 2 + z_lo), core: 2. Of those that a mesh axis runs over, the one named last changes fastest.
Arguments:
- labels: int32 [256, 128, 128], P('gz'), may hold values from 0 to 7
- label_table: float32 [8, 5], replicated, may hold values from 0.1 to 1.5
- spectra: float32 [32, 6], P('wl'), may hold values from 0.2 to 2
- illumination: int32 [128, 128], replicated, may hold values 0 or 1
- fluence_start: float32 [32, 256, 128, 128], P('wl', 'gz'), as said below
- measured: float32 [32, 256, 128, 128], P('wl', 'gz'), may hold values from 0 to 2
Outputs:
- fluence: float32 [32, 256, 128, 128], P('wl', 'gz')
- concentrations: float32 [4, 256, 128, 128], P(None, 'gz')
- scattering: float32 [256, 128, 128], P('gz')
The draws below stay inside these ranges and needn't reach their ends.
Inputs may be any that keep to these rules, and one draw needn't show every extreme that they name: `fluence_start`: positive, of order one.
All inputs are finite; a program needn't handle non-finite values.
Results may differ from the reference program's by a relative error of at most 0.0003.
Values sent between devices are 32-bit elements; how exact they have to be, the bound alone decides.
No kernel may reach another device: no remote copies, remote signals or barrier semaphores. Data moves between devices by JAX's collectives and lax.ppermute only.
A program may use at most 128 MiB of HBM per device.

```python
import math
import jax
import jax.numpy as jnp
from jax import lax

WAVES = 32
CHROMO = 4
LABELS = 8
ITERS = 2
NY = 128
NX = 128
NZ = 256
CELLS = 4194304


def draw_fluence_start(key, part):
    key = jax.random.fold_in(key, 11)
    depth = jnp.arange(NZ, dtype=jnp.float32) / max(NZ - 1, 1)
    shape = (WAVES, NZ, NY, NX)
    rough = jnp.exp(jax.random.uniform(key, shape, jnp.float32, math.log(0.3), math.log(3.0)))
    decay = jnp.exp(-math.log(3.0) * depth)
    return rough * decay[None, :, None, None]


def set_ends(entries, own_key, low, high):
    longest = entries.shape.index(max(entries.shape))
    spots = []
    for shift in (0, 1):
        where = [jax.random.randint(jax.random.fold_in(own_key, axis), (), 0, length) for axis, length in enumerate(entries.shape)]
        where[longest] = (where[longest] + shift) % entries.shape[longest]
        spots.append(tuple(where))
    return entries.at[spots[0]].set(low).at[spots[1]].set(high)


def level_of(stream_key, extent, shards, least, top_value):
    factor_of = 1.0
    for dim, parts in shards:
        draws = jax.random.uniform(jax.random.fold_in(jax.random.fold_in(stream_key, 6), dim), (parts,), jnp.float32, least / len(shards), top_value / len(shards))
        factor_of = factor_of * jnp.repeat(jnp.exp(draws), extent[dim] // parts).reshape((-1,) + (1,) * (len(extent) - 1 - dim))
    return factor_of


def setup_inputs(seed: int = 0) -> dict:
    streams_of = jax.random.split(jax.random.key(seed), 7)
    labels = set_ends(jax.random.randint(streams_of[0], (NZ, NY, NX), 0, LABELS), jax.random.fold_in(streams_of[0], 1), 0, LABELS - 1).astype(jnp.int32)
    label_table = jnp.clip(jnp.exp(jax.random.uniform(streams_of[1], (LABELS, CHROMO + 1), jnp.float32, math.log(0.1), math.log(1.5))), 0.1, 1.5)
    spectra = jnp.clip(jnp.exp(math.log(2.0) - 2.3025851 * jax.random.uniform(streams_of[2], (WAVES, CHROMO + 2), jnp.float32) ** level_of(streams_of[2], (WAVES, CHROMO + 2), ((0, 8),), -0.2, 0.2)), 0.2, 2.0)
    illumination = set_ends((jax.random.randint(streams_of[3], (NY, NX), 0, 2) < 1).astype(jnp.int32), jax.random.fold_in(streams_of[3], 1), 0, 1)
    fluence_start = draw_fluence_start(jax.random.fold_in(streams_of[6], 71), 0)
    measured = jnp.clip(2.0 * jax.random.uniform(streams_of[5], (WAVES, NZ, NY, NX), jnp.float32) ** level_of(streams_of[5], (WAVES, NZ, NY, NX), ((0, 8), (1, 32)), -0.2, 0.2), 0.0, 2.0)
    return dict(labels=labels, label_table=label_table, spectra=spectra, illumination=illumination, fluence_start=fluence_start, measured=measured)


eta_step = 0.3

def neighbours(padded):
    center = padded[:, 1:-1]
    ypadded = jnp.pad(center, ((0, 0), (0, 0), (1, 1), (0, 0)))
    xpadded = jnp.pad(center, ((0, 0), (0, 0), (0, 0), (1, 1)))
    return [padded[:, 2:], padded[:, :-2], ypadded[:, :, 2:], ypadded[:, :, :-2], xpadded[:, :, :, 2:], xpadded[:, :, :, :-2]]

def optics(spectra, coeffs):
    absorb = spectra[:, 0, None, None, None] * coeffs[0][None]
    for chrom in range(1, 4):
        absorb = absorb + spectra[:, chrom, None, None, None] * coeffs[chrom][None]
    diffuse = 1.0 / (3.0 * (absorb + spectra[:, 4, None, None, None] * coeffs[4][None]))
    return (absorb, diffuse)

def face_weights(diffuse_pad):
    center = diffuse_pad[:, 1:-1]
    return [0.5 * (center + other) for other in neighbours(diffuse_pad)]

def sweep(padded, weights, total, rhs):
    accum = rhs
    for weight, other in zip(weights, neighbours(padded)):
        accum = accum + weight * other
    return accum / total

def zpad(field):
    return jnp.pad(field, ((0, 0), (1, 1), (0, 0), (0, 0)))

def reference(labels, label_table, spectra, illumination, fluence_start, measured):
    coeffs = jnp.moveaxis(label_table[labels], -1, 0)
    absorb, diffuse = optics(spectra, coeffs)
    weights = face_weights(zpad(diffuse))
    total = absorb
    for weight in weights:
        total = total + weight
    source = spectra[:, 5, None, None, None] * illumination.astype(jnp.float32)[None, None]
    fluence = fluence_start
    for step in range(ITERS):
        fluence = sweep(zpad(fluence), weights, total, source)
    misfit = absorb * fluence - measured
    adjoint = jnp.zeros_like(fluence)
    for step in range(ITERS):
        adjoint = sweep(zpad(adjoint), weights, total, absorb * misfit)
    common = fluence * (misfit - adjoint)
    grads = [lax.optimization_barrier(jnp.sum(spectra[:, chrom, None, None, None] * common, axis=0)) for chrom in range(4)]
    flu_nb = neighbours(zpad(fluence))
    adj_nb = neighbours(zpad(adjoint))
    coupling = jnp.zeros_like(fluence)
    for weight, fother, aother in zip(weights, flu_nb, adj_nb):
        coupling = coupling + weight * (fother - fluence) * (aother - adjoint)
    grads.append(lax.optimization_barrier(jnp.sum(spectra[:, 4, None, None, None] * 3.0 * diffuse * diffuse * coupling, axis=0)))
    grad = jnp.stack(grads)
    rms = jnp.sqrt(lax.optimization_barrier(jnp.sum(grad * grad, axis=(1, 2, 3))) / CELLS + 1e-06)
    updated = coeffs * jnp.exp(-eta_step * grad / rms[:, None, None, None])
    return (fluence, updated[:4], updated[4])
```

```python
import functools

import jax
import jax.numpy as jnp
from jax import lax
from jax.experimental import pallas as pl
from jax.experimental.pallas import tpu as pltpu
from jax.sharding import PartitionSpec as P

STEP = 0.3
HF = 4
HM = 2
NP = 8
EXT = NP + 2 * HF
N = 128
F32 = jnp.float32

GENS = (2, 6, 1)
ORDERS = ((0, 1, 2), (1, 2, 0), (2, 0, 1))
PARTS = ((0, 14), (14, 27), (27, 40))
ROWS = 16


def code_of(part, slot):
    order = ORDERS[part]
    bits = (slot >> 2 & 1, slot >> 1 & 1, slot & 1)
    code = 0
    for dim, bit in zip(order, bits):
        code ^= GENS[dim] * bit
    return code


def slot_of(part, code):
    return [code_of(part, slot) for slot in range(8)].index(code)


def part_of(plane, field):
    at = plane * 5 + field
    for part, (first, last) in enumerate(PARTS):
        if at < last:
            return part, at - first


def ahead(x, axis):
    return pltpu.roll(x, N - 1, axis)


def behind(x, axis):
    return pltpu.roll(x, 1, axis)


def pick(classes, entries):
    bit0 = (classes & 1) != 0
    bit1 = (classes & 2) != 0
    bit2 = (classes & 4) != 0
    low = [jnp.where(bit0, entries[2 * i + 1], entries[2 * i]) for i in range(4)]
    mid = [jnp.where(bit1, low[2 * i + 1], low[2 * i]) for i in range(2)]
    return jnp.where(bit2, mid[1], mid[0])


def gather_faces(v, above, below, wx, wy, wabove, wbelow):
    return (
        wabove * above
        + wbelow * below
        + wy * ahead(v, 0)
        + behind(wy * v, 0)
        + wx * ahead(v, 1)
        + behind(wx * v, 1)
    )


def solve_kernel(
    where, spectra, absorb_t, half_t,
    labels, labels_a, labels_b, illum, start, start_a, start_b, meas, meas_a, meas_b,
    fluence, *rest,
):
    outs = rest[:6]
    cls, fl, hd, ab, wxs, wys, inv, tmp, mis, adj, ms, sem = rest[6:]
    sends, keeps = outs[0::2], outs[1::2]
    gz = where[0]
    me = where[1]
    odd = lax.rem(gz, 2)
    at_a = (1 - odd) * (HF + NP)
    at_b = odd * (HF + NP)
    mat_a = (1 - odd) * (HM + NP)
    mat_b = odd * (HM + NP)
    copies = [
        pltpu.make_async_copy(labels, cls.at[pl.ds(HF, NP)], sem.at[0]),
        pltpu.make_async_copy(labels_a, cls.at[pl.ds(at_a, HF)], sem.at[1]),
        pltpu.make_async_copy(labels_b, cls.at[pl.ds(at_b, HF)], sem.at[2]),
        pltpu.make_async_copy(start, fl.at[:, pl.ds(HF, NP)], sem.at[3]),
        pltpu.make_async_copy(start_a, fl.at[:, pl.ds(at_a, HF)], sem.at[4]),
        pltpu.make_async_copy(start_b, fl.at[:, pl.ds(at_b, HF)], sem.at[5]),
        pltpu.make_async_copy(meas, ms.at[:, pl.ds(HM, NP)], sem.at[6]),
        pltpu.make_async_copy(meas_a, ms.at[:, pl.ds(mat_a, HM)], sem.at[7]),
        pltpu.make_async_copy(meas_b, ms.at[:, pl.ds(mat_b, HM)], sem.at[8]),
    ]
    for copy in copies:
        copy.start()
    row = lax.broadcasted_iota(jnp.int32, (N, N), 0)
    col = lax.broadcasted_iota(jnp.int32, (N, N), 1)
    notlast_x = (col < N - 1).astype(F32)
    notlast_y = (row < N - 1).astype(F32)
    outer = (
        (col == 0).astype(F32) + (col == N - 1).astype(F32)
        + (row == 0).astype(F32) + (row == N - 1).astype(F32)
    )
    for copy in copies[:3]:
        copy.wait()

    def inside(e):
        z = gz * NP + e - HF
        return jnp.where((z >= 0) & (z < 32 * NP), 1.0, 0.0).astype(F32)

    def optics(e, _):
        classes = cls[e]
        there = inside(e)
        for l in range(4):
            ab[l, e] = pick(classes, [absorb_t[l, i] for i in range(8)])
            hd[l, e] = pick(classes, [half_t[l, i] * there for i in range(8)])
        return 0

    lax.fori_loop(0, EXT, optics, 0)
    for copy in copies[3:6]:
        copy.wait()

    def per_plane(first, last, body):
        def outerloop(l, _):
            def innerloop(e, _):
                body(l, e)
                return 0

            lax.fori_loop(first, last, innerloop, 0)
            return 0

        lax.fori_loop(0, 4, outerloop, 0)

    def first(l, e):
        h = hd[l, e]
        wx = (h + ahead(h, 1)) * notlast_x
        wy = (h + ahead(h, 0)) * notlast_y
        above = h + hd[l, e + 1]
        below = h + hd[l, e - 1]
        total = ab[l, e] + above + below + wx + behind(wx, 1) + wy + behind(wy, 0) + h * outer
        r = inside(e) / total
        wxs[l, e] = wx
        wys[l, e] = wy
        inv[l, e] = r
        source = spectra[l, 5] * illum[...].astype(F32)
        moved = gather_faces(fl[l, e], fl[l, e + 1], fl[l, e - 1], wx, wy, above, below)
        tmp[l, e] = (source + moved) * r

    per_plane(1, EXT - 1, first)
    for copy in copies[6:]:
        copy.wait()

    def second(l, e):
        h = hd[l, e]
        above = h + hd[l, e + 1]
        below = h + hd[l, e - 1]
        source = spectra[l, 5] * illum[...].astype(F32)
        moved = gather_faces(tmp[l, e], tmp[l, e + 1], tmp[l, e - 1], wxs[l, e], wys[l, e], above, below)
        r = inv[l, e]
        f = (source + moved) * r
        fl[l, e] = f
        absorb = ab[l, e]
        misfit = absorb * f - ms[l, e - (HF - HM)]
        mis[l, e] = misfit
        adj[l, e] = absorb * misfit * r

    per_plane(2, EXT - 2, second)
    write = pltpu.make_async_copy(fl.at[:, pl.ds(HF, NP)], fluence, sem.at[0])
    write.start()

    def third(l, e):
        h = hd[l, e]
        above = h + hd[l, e + 1]
        below = h + hd[l, e - 1]
        moved = gather_faces(adj[l, e], adj[l, e + 1], adj[l, e - 1], wxs[l, e], wys[l, e], above, below)
        tmp[l, e] = (ab[l, e] * mis[l, e] + moved) * inv[l, e]

    per_plane(3, EXT - 3, third)

    def couple(l, e):
        h = hd[l, e]
        f = fl[l, e]
        a = tmp[l, e]
        qx = wxs[l, e] * (ahead(f, 1) - f) * (ahead(a, 1) - a)
        qy = wys[l, e] * (ahead(f, 0) - f) * (ahead(a, 0) - a)
        total = (
            qx + behind(qx, 1) + qy + behind(qy, 0) + h * outer * f * a
            + (h + hd[l, e + 1]) * (fl[l, e + 1] - f) * (tmp[l, e + 1] - a)
            + (h + hd[l, e - 1]) * (fl[l, e - 1] - f) * (tmp[l, e - 1] - a)
        )
        ab[l, e] = 12.0 * h * h * total

    per_plane(HF, HF + NP, couple)

    for code in range(8):
        at = pl.multiple_of((me ^ code) * ROWS, ROWS)
        rows = pl.ds(at, ROWS)
        for plane in range(NP):
            e = plane + HF
            common = [fl[l, e, rows] * (mis[l, e, rows] - tmp[l, e, rows]) for l in range(4)]
            paired = [ab[l, e, rows] for l in range(4)]
            for field in range(5):
                terms = common if field < 4 else paired
                value = spectra[0, field] * terms[0]
                for l in range(1, 4):
                    value = value + spectra[l, field] * terms[l]
                part, index = part_of(plane, field)
                slot = slot_of(part, code)
                if slot >= 4:
                    sends[part][slot - 4, index] = value
                else:
                    keeps[part][slot, index] = value
    write.wait()


def squares_kernel(*refs):
    keeps, recvs, owns, sums = refs[:3], refs[3:6], refs[6:9], refs[9]
    total = [jnp.zeros((8, N), F32) for _ in range(5)]
    for plane in range(NP):
        for field in range(5):
            part, index = part_of(plane, field)
            value = keeps[part][0, index] + recvs[part][0, index]
            owns[part][0, index] = value
            squared = value * value
            total[field] = total[field] + squared[:8] + squared[8:]
    rows = [jnp.sum(t, axis=0, keepdims=True) for t in total]
    sums[...] = jnp.concatenate(rows + [jnp.zeros((3, N), F32)], axis=0)


def final_kernel(where, table, sums, labels, *refs):
    pieces, conc, scat = refs[:12], refs[12], refs[13]
    me = where[1]
    cells = 32 * NP * N * N
    total = jnp.sum(sums[...], axis=1, keepdims=True)
    factor = jnp.broadcast_to(-STEP / jnp.sqrt(total / cells + 1e-06), (8, N))
    factors = [jnp.broadcast_to(factor[c : c + 1], (ROWS, N)) for c in range(5)]
    for code in range(8):
        at = pl.multiple_of((me ^ code) * ROWS, ROWS)
        rows = pl.ds(at, ROWS)
        for plane in range(NP):
            classes = labels[plane, rows]
            for field in range(5):
                part, index = part_of(plane, field)
                slot = slot_of(part, code)
                own, one, two, four = pieces[4 * part : 4 * part + 4]
                if slot == 0:
                    grad = own[0, index]
                elif slot == 1:
                    grad = one[0, index]
                elif slot < 4:
                    grad = two[slot - 2, index]
                else:
                    grad = four[slot - 4, index]
                coeff = pick(classes, [table[i, field] for i in range(8)])
                value = coeff * jnp.exp(grad * factors[field])
                if field < 4:
                    conc[field, plane, rows] = value
                else:
                    scat[plane, rows] = value


VMEM = pl.BlockSpec(memory_space=pltpu.VMEM)
SMEM = pl.BlockSpec(memory_space=pltpu.SMEM)
ANY = pl.BlockSpec(memory_space=pl.ANY)


def swap(x, code):
    return lax.ppermute(x, "wl", [(i, i ^ code) for i in range(8)])


ON_CHIP = [(i, i ^ 1) for i in range(32)]
OFF_CHIP = [(i, i + 1) for i in range(1, 31, 2)] + [(i + 1, i) for i in range(1, 31, 2)]


def halo(x, axis, width, odd):
    extent = x.shape[axis]
    high = extent - width
    a = lax.dynamic_slice_in_dim(x, jnp.where(odd == 0, high, 0), width, axis)
    b = lax.dynamic_slice_in_dim(x, jnp.where(odd == 0, 0, high), width, axis)
    return lax.ppermute(a, "gz", ON_CHIP), lax.ppermute(b, "gz", OFF_CHIP)


def shards(labels, label_table, spectra, illumination, fluence_start, measured):
    gz = lax.axis_index("gz")
    me = lax.axis_index("wl")
    odd = lax.rem(gz, 2)
    where = jnp.stack([gz, me]).astype(jnp.int32)
    labels_a, labels_b = halo(labels, 0, HF, odd)
    start_a, start_b = halo(fluence_start, 1, HF, odd)
    meas_a, meas_b = halo(measured, 1, HM, odd)

    absorb_t = spectra[:, 0, None] * label_table[None, :, 0]
    for c in range(1, 4):
        absorb_t = absorb_t + spectra[:, c, None] * label_table[None, :, c]
    half_t = 0.5 / (3.0 * (absorb_t + spectra[:, 4, None] * label_table[None, :, 4]))

    sizes = [last - first for first, last in PARTS]
    field = pltpu.VMEM((4, EXT, N, N), F32)
    out = pl.pallas_call(
        solve_kernel,
        out_shape=[jax.ShapeDtypeStruct((4, NP, N, N), F32)]
        + [jax.ShapeDtypeStruct((4, size, ROWS, N), F32) for size in sizes for _ in range(2)],
        in_specs=[SMEM] * 4 + [ANY] * 3 + [VMEM] + [ANY] * 6,
        out_specs=[ANY] + [VMEM] * 6,
        scratch_shapes=[pltpu.VMEM((EXT, N, N), jnp.int32)]
        + [field] * 9
        + [pltpu.VMEM((4, NP + 2 * HM, N, N), F32), pltpu.SemaphoreType.DMA((9,))],
        compiler_params=pltpu.CompilerParams(vmem_limit_bytes=56 * 2**20),
        name="solve",
    )(where, spectra, absorb_t, half_t, labels, labels_a, labels_b, illumination,
      fluence_start, start_a, start_b, measured, meas_a, meas_b)
    fluence = out[0]
    sends = list(out[1::2])
    keeps = list(out[2::2])
    for phase in range(2):
        recvs = [swap(sends[q], GENS[ORDERS[q][phase]]) for q in range(3)]
        half = keeps[0].shape[0] // 2
        sends = [keeps[q][half:] + recvs[q][half:] for q in range(3)]
        keeps = [keeps[q][:half] + recvs[q][:half] for q in range(3)]
    recvs = [swap(sends[q], GENS[ORDERS[q][2]]) for q in range(3)]
    *owns, sums = pl.pallas_call(
        squares_kernel,
        out_shape=[jax.ShapeDtypeStruct((1, size, ROWS, N), F32) for size in sizes]
        + [jax.ShapeDtypeStruct((8, N), F32)],
        in_specs=[VMEM] * 6,
        out_specs=[VMEM] * 4,
        name="squares",
    )(*keeps, *recvs)

    ones = [swap(owns[q], GENS[ORDERS[q][2]]) for q in range(3)]
    for code in (1, 2, 4, 8, 16):
        sums = sums + lax.ppermute(sums, "gz", [(i, i ^ code) for i in range(32)])
    pairs = [jnp.concatenate([owns[q], ones[q]]) for q in range(3)]
    twos = [swap(pairs[q], GENS[ORDERS[q][1]]) for q in range(3)]
    quads = [jnp.concatenate([pairs[q], twos[q]]) for q in range(3)]
    fours = [swap(quads[q], GENS[ORDERS[q][0]]) for q in range(3)]
    for code in GENS:
        sums = sums + swap(sums, code)
    pieces = []
    for q in range(3):
        pieces += [owns[q], ones[q], twos[q], fours[q]]
    conc, scat = pl.pallas_call(
        final_kernel,
        out_shape=[jax.ShapeDtypeStruct((4, NP, N, N), F32), jax.ShapeDtypeStruct((NP, N, N), F32)],
        in_specs=[SMEM] * 2 + [VMEM] * 14,
        out_specs=[VMEM] * 2,
        compiler_params=pltpu.CompilerParams(vmem_limit_bytes=32 * 2**20),
        name="final",
    )(where, label_table, sums, labels, *pieces)
    return fluence, conc, scat


def solution(mesh):
    in_specs = (
        P("gz", None, None),
        P(),
        P("wl", None),
        P(),
        P("wl", "gz", None, None),
        P("wl", "gz", None, None),
    )
    out_specs = (P("wl", "gz", None, None), P(None, "gz", None, None), P("gz", None, None))
    return jax.shard_map(shards, mesh=mesh, in_specs=in_specs, out_specs=out_specs, check_vma=False)
```

```python
import functools

import jax
import jax.numpy as jnp
from jax import lax
from jax.experimental import pallas as pl
from jax.experimental.pallas import tpu as pltpu
from jax.sharding import PartitionSpec as P

STEP = 0.3
HF = 3
HM = 1
NP = 8
EXT = NP + 2 * HF
N = 128
PAD = 8
CHUNK = 32
F32 = jnp.float32

GENS = (2, 6, 1)
ORDERS = ((0, 1, 2), (1, 2, 0), (2, 0, 1))
PARTS = ((0, 14), (14, 27), (27, 40))
ROWS = 16


def code_of(part, slot):
    order = ORDERS[part]
    bits = (slot >> 2 & 1, slot >> 1 & 1, slot & 1)
    code = 0
    for dim, bit in zip(order, bits):
        code ^= GENS[dim] * bit
    return code


def slot_of(part, code):
    return [code_of(part, slot) for slot in range(8)].index(code)


def part_of(plane, field):
    at = plane * 5 + field
    for part, (first, last) in enumerate(PARTS):
        if at < last:
            return part, at - first


def shifts():
    source = lax.broadcasted_iota(jnp.int32, (2 * N, 2 * N), 0)
    target = lax.broadcasted_iota(jnp.int32, (2 * N, 2 * N), 1)
    x = jnp.where(source >= N, source - N, source)
    ahead = (target < N) & (x == target + 1)
    behind = (target >= N) & (x == target - N - 1)
    return jnp.where(ahead | behind, 1.0, 0.0).astype(jnp.bfloat16)


def two_terms(v):
    high = v.astype(jnp.bfloat16)
    low = (v - high.astype(F32)).astype(jnp.bfloat16)
    return jnp.concatenate([high, low], axis=1)


def pick(classes, entries):
    bit0 = (classes & 1) != 0
    bit1 = (classes & 2) != 0
    bit2 = (classes & 4) != 0
    low = [jnp.where(bit0, entries[2 * i + 1], entries[2 * i]) for i in range(4)]
    mid = [jnp.where(bit1, low[2 * i + 1], low[2 * i]) for i in range(2)]
    return jnp.where(bit2, mid[1], mid[0])


def pack_kernel(where, labels, start, meas, side_a, side_b, ints, sem):
    odd = lax.rem(where[0], 2)
    high_f, high_m = NP - HF, NP - HM
    copies = []
    for at, (out, flip) in enumerate(((side_a, 1 - odd), (side_b, odd))):
        copies.append(pltpu.make_async_copy(labels.at[pl.ds(flip * high_f, HF)], ints.at[at], sem.at[at, 8]))
        for l in range(4):
            copies.append(
                pltpu.make_async_copy(
                    start.at[l, pl.ds(flip * high_f, HF)], out.at[pl.ds(l * HF, HF)], sem.at[at, l]
                )
            )
            copies.append(
                pltpu.make_async_copy(
                    meas.at[l, pl.ds(flip * high_m, HM)], out.at[pl.ds(4 * HF + l * HM, HM)], sem.at[at, 4 + l]
                )
            )
    for copy in copies:
        copy.start()
    for copy in copies:
        copy.wait()
    for at, out in enumerate((side_a, side_b)):
        out[4 * (HF + HM) : 4 * (HF + HM) + HF] = ints[at].astype(F32)


def solve_kernel(
    where, spectra, absorb_t, half_t, labels, illum, start, meas, side_a, side_b,
    fluence, coef_a, coef_b, edge_a, edge_b, *rest,
):
    outs = rest[:6]
    own, shared, lit, step, near, near2, fl, hd, wys, tmp, adj, ab, wes, wws, wzs, inv, mis, ms, sem = rest[6:]
    sends, keeps = outs[0::2], outs[1::2]
    gz = where[0]
    me = where[1]
    odd = lax.rem(gz, 2)
    whole = pl.ds(PAD, N)
    copies = [
        pltpu.make_async_copy(labels, own, sem.at[0]),
        pltpu.make_async_copy(start, fl.at[:, pl.ds(HF, NP), whole], sem.at[1]),
        pltpu.make_async_copy(meas, ms.at[:, pl.ds(HM, NP)], sem.at[2]),
    ]
    label_copies = []
    side_copies = []
    for at, (side, high) in enumerate(((side_a, 1 - odd), (side_b, odd))):
        f_at = high * (HF + NP)
        m_at = high * (HM + NP)
        label_copies.append(
            pltpu.make_async_copy(side.at[pl.ds(4 * (HF + HM), HF)], shared.at[pl.ds(high * HF, HF)], sem.at[3 + at])
        )
        for l in range(4):
            side_copies.append(
                pltpu.make_async_copy(
                    side.at[pl.ds(l * HF, HF)], fl.at[l, pl.ds(f_at, HF), whole], sem.at[5 + 8 * at + l]
                )
            )
            side_copies.append(
                pltpu.make_async_copy(
                    side.at[pl.ds(4 * HF + l * HM, HM)], ms.at[l, pl.ds(m_at, HM)], sem.at[9 + 8 * at + l]
                )
            )
    for copy in label_copies + copies + side_copies:
        copy.start()

    lit[...] = illum[...].astype(F32)
    step[...] = shifts()
    pad = jnp.zeros((PAD, N), F32)

    def inside(e):
        z = gz * NP + e - HF
        return jnp.where((z >= 0) & (z < 32 * NP), 1.0, 0.0).astype(F32)

    def clear(e, _):
        for l in range(4):
            for field in (fl, tmp, adj, hd):
                field[l, e, 0:PAD] = pad
                field[l, e, PAD + N : 2 * PAD + N] = pad
        return 0

    lax.fori_loop(0, EXT, clear, 0)

    def optics(classes, e, r):
        there = inside(e)
        flat = pl.ds(r, CHUNK)
        rows = pl.ds(PAD + r, CHUNK)
        for l in range(4):
            ab[l, e, flat] = pick(classes, [absorb_t[l, i] for i in range(8)])
            hd[l, e, rows] = pick(classes, [half_t[l, i] * there for i in range(8)])

    def optics_own(p, _):
        for c in range(N // CHUNK):
            optics(own[p, pl.ds(c * CHUNK, CHUNK)], p + HF, c * CHUNK)
        return 0

    def optics_shared(p, _):
        e = p + jnp.where(p < HF, 0, NP)
        for c in range(N // CHUNK):
            classes = shared[p, pl.ds(c * CHUNK, CHUNK)].astype(jnp.int32)
            optics(classes, e, c * CHUNK)
        return 0

    copies[0].wait()
    lax.fori_loop(0, NP, optics_own, 0)
    for copy in label_copies:
        copy.wait()
    lax.fori_loop(0, 2 * HF, optics_shared, 0)
    for copy in copies[1:] + side_copies:
        copy.wait()

    @pl.when(gz == 0)
    def _():
        fl[:, HF - 1] = jnp.zeros((4, N + 2 * PAD, N), F32)

    @pl.when(gz == 31)
    def _():
        fl[:, HF + NP] = jnp.zeros((4, N + 2 * PAD, N), F32)

    def spread(to, field, l, first, last):
        rows = field[l, first:last, PAD : PAD + N].reshape((last - first) * N, N)
        both = jnp.dot(two_terms(rows), step[...], preferred_element_type=F32)
        to[first:last] = both.reshape(last - first, N, 2 * N)

    def per_plane(first, last, fields, body):
        def outerloop(l, _):
            for to, field in zip((near, near2), fields):
                spread(to, field, l, first, last)

            def innerloop(e, _):
                for c in range(N // CHUNK):
                    body(l, e, c * CHUNK)
                return 0

            lax.fori_loop(first, last, innerloop, 0)
            return 0

        lax.fori_loop(0, 4, outerloop, 0)

    def moved(field, l, e, r):
        flat = pl.ds(r, CHUNK)
        here = pl.ds(PAD + r, CHUNK)
        north = pl.ds(PAD + r + 1, CHUNK)
        south = pl.ds(PAD + r - 1, CHUNK)
        return (
            wzs[l, e, flat] * field[l, e + 1, here]
            + wzs[l, e - 1, flat] * field[l, e - 1, here]
            + wys[l, e, here] * field[l, e, north]
            + wys[l, e, south] * field[l, e, south]
            + wes[l, e, flat] * near[e, flat, 0:N]
            + wws[l, e, flat] * near[e, flat, N : 2 * N]
        )

    for l in range(4):
        for c in range(N // CHUNK):
            here = pl.ds(PAD + c * CHUNK, CHUNK)
            wzs[l, 0, pl.ds(c * CHUNK, CHUNK)] = hd[l, 0, here] + hd[l, 1, here]

    def first(l, e, r):
        flat = pl.ds(r, CHUNK)
        here = pl.ds(PAD + r, CHUNK)
        north_rows = pl.ds(PAD + r + 1, CHUNK)
        south_rows = pl.ds(PAD + r - 1, CHUNK)
        h = hd[l, e, here]
        north = h + hd[l, e, north_rows]
        south = h + hd[l, e, south_rows]
        above = h + hd[l, e + 1, here]
        below = wzs[l, e - 1, flat]
        east = h + near2[e, flat, 0:N]
        west = h + near2[e, flat, N : 2 * N]
        if r == 0:
            wys[l, e, 0:PAD] = jnp.broadcast_to(h[0:1], (PAD, N))
        wys[l, e, here] = north
        wzs[l, e, flat] = above
        wes[l, e, flat] = east
        wws[l, e, flat] = west
        total = ab[l, e, flat] + above + below + north + south + east + west
        scale = inside(e) / total
        inv[l, e, flat] = scale
        flow = (
            above * fl[l, e + 1, here]
            + below * fl[l, e - 1, here]
            + north * fl[l, e, north_rows]
            + south * fl[l, e, south_rows]
            + east * near[e, flat, 0:N]
            + west * near[e, flat, N : 2 * N]
        )
        tmp[l, e, here] = (spectra[l, 5] * lit[flat] + flow) * scale

    per_plane(1, EXT - 1, (fl, hd), first)

    def second(l, e, r):
        flat = pl.ds(r, CHUNK)
        here = pl.ds(PAD + r, CHUNK)
        scale = inv[l, e, flat]
        f = (spectra[l, 5] * lit[flat] + moved(tmp, l, e, r)) * scale
        fl[l, e, here] = f
        absorb = ab[l, e, flat]
        misfit = absorb * f - ms[l, e - (HF - HM), flat]
        mis[l, e, flat] = misfit
        adj[l, e, here] = absorb * misfit * scale

    per_plane(2, EXT - 2, (tmp,), second)
    write = pltpu.make_async_copy(fl.at[:, pl.ds(HF, NP), whole], fluence, sem.at[0])
    write.start()
    for l in range(4):
        tmp[l, HF - 1] = jnp.zeros((N + 2 * PAD, N), F32)
        tmp[l, HF + NP] = jnp.zeros((N + 2 * PAD, N), F32)

    def third(l, e, r):
        flat = pl.ds(r, CHUNK)
        here = pl.ds(PAD + r, CHUNK)
        tmp[l, e, here] = (ab[l, e, flat] * mis[l, e, flat] + moved(adj, l, e, r)) * inv[l, e, flat]

    per_plane(HF, HF + NP, (adj,), third)

    def couple(l, e, r):
        flat = pl.ds(r, CHUNK)
        here = pl.ds(PAD + r, CHUNK)
        north = pl.ds(PAD + r + 1, CHUNK)
        south = pl.ds(PAD + r - 1, CHUNK)
        h = hd[l, e, here]
        f = fl[l, e, here]
        a = tmp[l, e, here]
        total = (
            wes[l, e, flat] * (near[e, flat, 0:N] - f) * (near2[e, flat, 0:N] - a)
            + wws[l, e, flat] * (near[e, flat, N : 2 * N] - f) * (near2[e, flat, N : 2 * N] - a)
            + wys[l, e, here] * (fl[l, e, north] - f) * (tmp[l, e, north] - a)
            + wys[l, e, south] * (fl[l, e, south] - f) * (tmp[l, e, south] - a)
            + wzs[l, e, flat] * (fl[l, e + 1, here] - f) * (tmp[l, e + 1, here] - a)
            + wzs[l, e - 1, flat] * (fl[l, e - 1, here] - f) * (tmp[l, e - 1, here] - a)
        )
        ab[l, e, flat] = 12.0 * h * h * total

    per_plane(HF, HF + NP, (fl, tmp), couple)

    for coef, edge, high in ((coef_a, edge_a, 1 - odd), (coef_b, edge_b, odd)):
        e = HF + high * (NP - 1)
        beyond = e + 2 * high - 1
        face = e + high - 1
        for l in range(4):
            for c in range(N // CHUNK):
                here = pl.ds(PAD + c * CHUNK, CHUNK)
                to = pl.ds(c * CHUNK, CHUNK)
                h = hd[l, e, here]
                edge[l, to] = tmp[l, e, here]
                coef[l, to] = (
                    spectra[l, 4] * 12.0 * h * h * wzs[l, face, to] * (fl[l, beyond, here] - fl[l, e, here])
                )

    for code in range(8):
        rows = pl.ds(pl.multiple_of(PAD + (me ^ code) * ROWS, 8), ROWS)
        flat = pl.ds(pl.multiple_of((me ^ code) * ROWS, 8), ROWS)
        for plane in range(NP):
            e = plane + HF
            common = [fl[l, e, rows] * (mis[l, e, flat] - tmp[l, e, rows]) for l in range(4)]
            paired = [ab[l, e, flat] for l in range(4)]
            for field in range(5):
                terms = common if field < 4 else paired
                value = spectra[0, field] * terms[0]
                for l in range(1, 4):
                    value = value + spectra[l, field] * terms[l]
                part, index = part_of(plane, field)
                slot = slot_of(part, code)
                if slot >= 4:
                    sends[part][slot - 4, index] = value
                else:
                    keeps[part][slot, index] = value
    write.wait()


def edge_kernel(where, coef_a, coef_b, edge_a, edge_b, send, keep):
    gz, me = where[0], where[1]
    there = jnp.where((gz > 0) & (gz < 31), 1.0, 0.0).astype(F32)
    for code in range(8):
        rows = pl.ds(pl.multiple_of((me ^ code) * ROWS, ROWS), ROWS)
        slot = slot_of(0, code)
        for side, (coef, edge) in enumerate(((coef_a, edge_a), (coef_b, edge_b))):
            value = coef[0, rows] * edge[0, rows]
            for l in range(1, 4):
                value = value + coef[l, rows] * edge[l, rows]
            if side:
                value = value * there
            if slot >= 4:
                send[slot - 4, side] = value
            else:
                keep[slot, side] = value


def squares_kernel(where, late_keep, late_recv, *refs):
    keeps, recvs, owns, sums = refs[:3], refs[3:6], refs[6:9], refs[9]
    odd = lax.rem(where[0], 2)
    total = [jnp.zeros((8, N), F32) for _ in range(5)]
    for plane in range(NP):
        for field in range(5):
            part, index = part_of(plane, field)
            value = keeps[part][0, index] + recvs[part][0, index]
            if field == 4 and plane in (0, NP - 1):
                side = 1 - odd if plane == 0 else odd
                value = value + (late_keep[0, side] + late_recv[0, side])
            owns[part][0, index] = value
            squared = value * value
            total[field] = total[field] + squared[:8] + squared[8:]
    lane = lax.broadcasted_iota(jnp.int32, (1, N), 1)
    row = jnp.zeros((1, N), F32)
    for field in range(5):
        whole = jnp.sum(jnp.sum(total[field], axis=0, keepdims=True), axis=1, keepdims=True)
        row = jnp.where(lane == field, whole, row)
    for target in range(32):
        sums[target] = row


def final_kernel(where, table, labels, *refs):
    pieces, conc, scat = refs[:12], refs[12], refs[13]
    me = where[1]
    cells = 32 * NP * N * N
    extra = PARTS[0][1]
    total = pieces[0][0, extra] + pieces[1][0, extra]
    for i in range(2):
        total = total + pieces[2][i, extra]
    for i in range(4):
        total = total + pieces[3][i, extra]
    factor = -STEP / jnp.sqrt(total / cells + 1e-06)
    factors = [jnp.broadcast_to(factor[:, c : c + 1], (ROWS, N)) for c in range(5)]
    for code in range(8):
        at = pl.multiple_of((me ^ code) * ROWS, ROWS)
        rows = pl.ds(at, ROWS)
        for plane in range(NP):
            classes = labels[plane, rows]
            for field in range(5):
                part, index = part_of(plane, field)
                slot = slot_of(part, code)
                own, one, two, four = pieces[4 * part : 4 * part + 4]
                if slot == 0:
                    grad = own[0, index]
                elif slot == 1:
                    grad = one[0, index]
                elif slot < 4:
                    grad = two[slot - 2, index]
                else:
                    grad = four[slot - 4, index]
                coeff = pick(classes, [table[i, field] for i in range(8)])
                value = coeff * jnp.exp(grad * factors[field])
                if field < 4:
                    conc[field, plane, rows] = value
                else:
                    scat[plane, rows] = value


VMEM = pl.BlockSpec(memory_space=pltpu.VMEM)
SMEM = pl.BlockSpec(memory_space=pltpu.SMEM)
ANY = pl.BlockSpec(memory_space=pl.ANY)


def swap(x, code):
    return lax.ppermute(x, "wl", [(i, i ^ code) for i in range(8)])


ON_CHIP = [(i, i ^ 1) for i in range(32)]
OFF_CHIP = [(i, (i + 1 if i % 2 else i - 1) % 32) for i in range(32)]


def beside(a, b):
    return lax.ppermute(a, "gz", ON_CHIP), lax.ppermute(b, "gz", OFF_CHIP)


def after(x, *others):
    return lax.optimization_barrier((x, *others))[0]


def shards(labels, label_table, spectra, illumination, fluence_start, measured):
    where = jnp.stack([lax.axis_index("gz"), lax.axis_index("wl")]).astype(jnp.int32)
    packed = 4 * (HF + HM) + HF
    side_a, side_b = pl.pallas_call(
        pack_kernel,
        out_shape=[jax.ShapeDtypeStruct((packed, N, N), F32)] * 2,
        in_specs=[SMEM] + [ANY] * 3,
        out_specs=[VMEM] * 2,
        scratch_shapes=[pltpu.VMEM((2, HF, N, N), jnp.int32), pltpu.SemaphoreType.DMA((2, 9))],
        name="pack",
    )(where, labels, fluence_start, measured)
    side_a, side_b = beside(side_a, side_b)

    absorb_t = spectra[:, 0, None] * label_table[None, :, 0]
    for c in range(1, 4):
        absorb_t = absorb_t + spectra[:, c, None] * label_table[None, :, c]
    half_t = 0.5 / (3.0 * (absorb_t + spectra[:, 4, None] * label_table[None, :, 4]))

    sizes = [last - first for first, last in PARTS]
    field = pltpu.VMEM((4, EXT, N + 2 * PAD, N), F32)
    plane = jax.ShapeDtypeStruct((4, N, N), F32)
    fluence, coef_a, coef_b, edge_a, edge_b, *out = pl.pallas_call(
        solve_kernel,
        out_shape=[jax.ShapeDtypeStruct((4, NP, N, N), F32)]
        + [plane] * 4
        + [jax.ShapeDtypeStruct((4, size, ROWS, N), F32) for size in sizes for _ in range(2)],
        in_specs=[SMEM] * 4 + [ANY] + [VMEM] + [ANY] * 4,
        out_specs=[ANY] + [VMEM] * 10,
        scratch_shapes=[
            pltpu.VMEM((NP, N, N), jnp.int32),
            pltpu.VMEM((2 * HF, N, N), F32),
            pltpu.VMEM((N, N), F32),
            pltpu.VMEM((2 * N, 2 * N), jnp.bfloat16),
        ]
        + [pltpu.VMEM((EXT, N, 2 * N), F32)] * 2
        + [field] * 5
        + [pltpu.VMEM((4, EXT, N, N), F32)] * 6
        + [pltpu.VMEM((4, NP + 2 * HM, N, N), F32), pltpu.SemaphoreType.DMA((21,))],
        compiler_params=pltpu.CompilerParams(vmem_limit_bytes=57 * 2**20),
        name="solve",
    )(where, spectra, absorb_t, half_t, labels, illumination, fluence_start, measured, side_a, side_b)
    sends = list(out[0::2])
    keeps = list(out[1::2])

    far_a, far_b = beside(edge_a, edge_b)
    for phase in range(2):
        recvs = [swap(sends[q], GENS[ORDERS[q][phase]]) for q in range(3)]
        half = keeps[0].shape[0] // 2
        sends = [keeps[q][half:] + recvs[q][half:] for q in range(3)]
        keeps = [keeps[q][:half] + recvs[q][:half] for q in range(3)]
        if phase == 0:
            far_a, far_b = lax.optimization_barrier((far_a, far_b, *sends))[:2]
    recvs = [swap(sends[q], GENS[ORDERS[q][2]]) for q in range(3)]

    late_send, late_keep = pl.pallas_call(
        edge_kernel,
        out_shape=[jax.ShapeDtypeStruct((4, 2, ROWS, N), F32)] * 2,
        in_specs=[SMEM] + [VMEM] * 4,
        out_specs=[VMEM] * 2,
        name="edge",
    )(where, coef_a, coef_b, far_a, far_b)
    for phase in range(2):
        late_recv = swap(late_send, GENS[ORDERS[0][phase]])
        half = late_keep.shape[0] // 2
        late_send = late_keep[half:] + late_recv[half:]
        late_keep = late_keep[:half] + late_recv[:half]
    late_recv = swap(late_send, GENS[ORDERS[0][2]])

    *owns, sums = pl.pallas_call(
        squares_kernel,
        out_shape=[jax.ShapeDtypeStruct((1, size, ROWS, N), F32) for size in sizes]
        + [jax.ShapeDtypeStruct((32, 1, N), F32)],
        in_specs=[SMEM] + [VMEM] * 8,
        out_specs=[VMEM] * 4,
        name="squares",
    )(where, late_keep, late_recv, *keeps, *recvs)

    steps = {q: [owns[q]] for q in (1, 2)}
    for phase in (2, 1, 0):
        for q in (1, 2):
            have = steps[q]
            mine = have[0] if len(have) == 1 else jnp.concatenate(have)
            have.append(swap(mine, GENS[ORDERS[q][phase]]))
    slab = jnp.sum(lax.all_to_all(sums, "gz", 0, 0), axis=0)
    steps[0] = [jnp.concatenate([owns[0], jnp.broadcast_to(slab[None, None], (1, 1, ROWS, N))], axis=1)]
    for phase in (2, 1, 0):
        have = steps[0]
        mine = have[0] if len(have) == 1 else jnp.concatenate(have)
        have.append(swap(mine, GENS[ORDERS[0][phase]]))
    pieces = steps[0] + steps[1] + steps[2]
    conc, scat = pl.pallas_call(
        final_kernel,
        out_shape=[jax.ShapeDtypeStruct((4, NP, N, N), F32), jax.ShapeDtypeStruct((NP, N, N), F32)],
        in_specs=[SMEM] * 2 + [VMEM] * 13,
        out_specs=[VMEM] * 2,
        compiler_params=pltpu.CompilerParams(vmem_limit_bytes=32 * 2**20),
        name="final",
    )(where, label_table, labels, *pieces)
    return fluence, conc, scat


def solution(mesh):
    in_specs = (
        P("gz", None, None),
        P(),
        P("wl", None),
        P(),
        P("wl", "gz", None, None),
        P("wl", "gz", None, None),
    )
    out_specs = (P("wl", "gz", None, None), P(None, "gz", None, None), P("gz", None, None))
    return jax.shard_map(shards, mesh=mesh, in_specs=in_specs, out_specs=out_specs, check_vma=False)
```

```python
import functools

import jax
import jax.numpy as jnp
from jax import lax
from jax.experimental import pallas as pl
from jax.experimental.pallas import tpu as pltpu
from jax.sharding import PartitionSpec as P

STEP = 0.3
HF = 3
HM = 1
NP = 8
EXT = NP + 2 * HF
N = 128
PAD = 8
CHUNK = 32
F32 = jnp.float32

GENS = (2, 6, 1)
ORDERS = ((0, 1, 2), (1, 2, 0), (2, 0, 1))
PARTS = ((0, 14), (14, 27), (27, 40))
ROWS = 16


def code_of(part, slot):
    order = ORDERS[part]
    bits = (slot >> 2 & 1, slot >> 1 & 1, slot & 1)
    code = 0
    for dim, bit in zip(order, bits):
        code ^= GENS[dim] * bit
    return code


def slot_of(part, code):
    return [code_of(part, slot) for slot in range(8)].index(code)


def part_of(plane, field):
    at = plane * 5 + field
    for part, (first, last) in enumerate(PARTS):
        if at < last:
            return part, at - first


def shifts():
    source = lax.broadcasted_iota(jnp.int32, (2 * N, 2 * N), 0)
    target = lax.broadcasted_iota(jnp.int32, (2 * N, 2 * N), 1)
    x = jnp.where(source >= N, source - N, source)
    ahead = (target < N) & (x == target + 1)
    behind = (target >= N) & (x == target - N - 1)
    return jnp.where(ahead | behind, 1.0, 0.0).astype(jnp.bfloat16)


def two_terms(v):
    high = v.astype(jnp.bfloat16)
    low = (v - high.astype(F32)).astype(jnp.bfloat16)
    return jnp.concatenate([high, low], axis=1)


def pick(classes, entries):
    bit0 = (classes & 1) != 0
    bit1 = (classes & 2) != 0
    bit2 = (classes & 4) != 0
    low = [jnp.where(bit0, entries[2 * i + 1], entries[2 * i]) for i in range(4)]
    mid = [jnp.where(bit1, low[2 * i + 1], low[2 * i]) for i in range(2)]
    return jnp.where(bit2, mid[1], mid[0])


def pack_kernel(high, labels, start, meas, *rest):
    *outs, ints, sem = rest
    bulk, extra = outs[0], outs[-1]
    at = 4 * HF if len(outs) == 1 else 0
    flip = high[0]
    copies = [pltpu.make_async_copy(labels.at[pl.ds(flip * (NP - HF), HF)], ints, sem.at[8])]
    for l in range(4):
        copies.append(
            pltpu.make_async_copy(start.at[l, pl.ds(flip * (NP - HF), HF)], bulk.at[pl.ds(l * HF, HF)], sem.at[l])
        )
        copies.append(
            pltpu.make_async_copy(
                meas.at[l, pl.ds(flip * (NP - HM), HM)], extra.at[pl.ds(at + l * HM, HM)], sem.at[4 + l]
            )
        )
    for copy in copies:
        copy.start()
    for copy in copies:
        copy.wait()
    extra[at + 4 * HM : at + 4 * HM + HF] = ints[...].astype(F32)


def solve_kernel(
    where, spectra, absorb_t, half_t, labels, illum, start, meas, side_a, bulk_b, straight_b, turned_b,
    fluence, coef_a, coef_b, edge_a, edge_b, *rest,
):
    outs = rest[:6]
    own, shared, lit, step, near, near2, fl, hd, wys, tmp, adj, ab, wes, wws, wzs, inv, ms, sem = rest[6:]
    sends, keeps = outs[0::2], outs[1::2]
    gz = where[0]
    me = where[1]
    odd = lax.rem(gz, 2)
    whole = pl.ds(PAD, N)
    copies = [
        pltpu.make_async_copy(labels, own, sem.at[0]),
        pltpu.make_async_copy(start, fl.at[:, pl.ds(HF, NP), whole], sem.at[1]),
        pltpu.make_async_copy(meas, ms.at[:, pl.ds(HM, NP)], sem.at[2]),
    ]

    def extras(side, at, high, number):
        first = 3 + 5 * number
        return [
            pltpu.make_async_copy(
                side.at[pl.ds(at + 4 * HM, HF)], shared.at[pl.ds(high * HF, HF)], sem.at[first]
            )
        ] + [
            pltpu.make_async_copy(
                side.at[pl.ds(at + l * HM, HM)], ms.at[l, pl.ds(high * (HM + NP), HM)], sem.at[first + 1 + l]
            )
            for l in range(4)
        ]

    extras_a = extras(side_a, 4 * HF, 1 - odd, 0)
    extras_b = extras(straight_b, 0, odd, 1)
    label_copies = [extras_a[0], extras_b[0]]
    meas_copies = [copies[2]] + extras_a[1:] + extras_b[1:]
    fluence_copies = [copies[1]] + [
        pltpu.make_async_copy(
            side.at[pl.ds(l * HF, HF)],
            fl.at[l, pl.ds(high * (HF + NP), HF), whole],
            sem.at[13 + 4 * number + l],
        )
        for number, (side, high) in enumerate(((side_a, 1 - odd), (bulk_b, odd)))
        for l in range(4)
    ]
    turned = (lax.rem(gz, 8) == 0) | (lax.rem(gz, 8) == 7)
    copies[0].start()
    extras_a[0].start()

    @pl.when(turned)
    def _():
        for copy in extras(turned_b, 0, odd, 1):
            copy.start()

    @pl.when(jnp.logical_not(turned))
    def _():
        for copy in extras_b:
            copy.start()

    for copy in fluence_copies + [copies[2]] + extras_a[1:]:
        copy.start()

    lit[...] = illum[...].astype(F32)
    step[...] = shifts()
    pad = jnp.zeros((PAD, N), F32)

    def inside(e):
        z = gz * NP + e - HF
        return jnp.where((z >= 0) & (z < 32 * NP), 1.0, 0.0).astype(F32)

    def clear(e, _):
        for l in range(4):
            for field in (fl, tmp, adj, hd):
                field[l, e, 0:PAD] = pad
                field[l, e, PAD + N : 2 * PAD + N] = pad
        return 0

    lax.fori_loop(0, EXT, clear, 0)

    def optics(classes, e, r):
        there = inside(e)
        flat = pl.ds(r, CHUNK)
        rows = pl.ds(PAD + r, CHUNK)
        for l in range(4):
            ab[l, e, flat] = pick(classes, [absorb_t[l, i] for i in range(8)])
            hd[l, e, rows] = pick(classes, [half_t[l, i] * there for i in range(8)])

    def optics_own(p, _):
        for c in range(N // CHUNK):
            optics(own[p, pl.ds(c * CHUNK, CHUNK)], p + HF, c * CHUNK)
        return 0

    def optics_shared(p, _):
        e = p + jnp.where(p < HF, 0, NP)
        for c in range(N // CHUNK):
            classes = shared[p, pl.ds(c * CHUNK, CHUNK)].astype(jnp.int32)
            optics(classes, e, c * CHUNK)
        return 0

    copies[0].wait()
    lax.fori_loop(0, NP, optics_own, 0)
    for copy in label_copies:
        copy.wait()
    lax.fori_loop(0, 2 * HF, optics_shared, 0)
    for copy in fluence_copies:
        copy.wait()

    @pl.when(gz == 0)
    def _():
        fl[:, HF - 1] = jnp.zeros((4, N + 2 * PAD, N), F32)

    @pl.when(gz == 31)
    def _():
        fl[:, HF + NP] = jnp.zeros((4, N + 2 * PAD, N), F32)

    def spread(to, field, l, first, last):
        rows = field[l, first:last, PAD : PAD + N].reshape((last - first) * N, N)
        both = jnp.dot(two_terms(rows), step[...], preferred_element_type=F32)
        to[first:last] = both.reshape(last - first, N, 2 * N)

    def per_plane(first, last, fields, body):
        def outerloop(l, _):
            for to, field in zip((near, near2), fields):
                spread(to, field, l, first, last)

            def innerloop(e, _):
                for c in range(N // CHUNK):
                    body(l, e, c * CHUNK)
                return 0

            lax.fori_loop(first, last, innerloop, 0)
            return 0

        lax.fori_loop(0, 4, outerloop, 0)

    def moved(field, l, e, r):
        flat = pl.ds(r, CHUNK)
        here = pl.ds(PAD + r, CHUNK)
        north = pl.ds(PAD + r + 1, CHUNK)
        south = pl.ds(PAD + r - 1, CHUNK)
        return (
            wzs[l, e, flat] * field[l, e + 1, here]
            + wzs[l, e - 1, flat] * field[l, e - 1, here]
            + wys[l, e, here] * field[l, e, north]
            + wys[l, e, south] * field[l, e, south]
            + wes[l, e, flat] * near[e, flat, 0:N]
            + wws[l, e, flat] * near[e, flat, N : 2 * N]
        )

    for l in range(4):
        for c in range(N // CHUNK):
            here = pl.ds(PAD + c * CHUNK, CHUNK)
            wzs[l, 0, pl.ds(c * CHUNK, CHUNK)] = hd[l, 0, here] + hd[l, 1, here]

    def first(l, e, r):
        flat = pl.ds(r, CHUNK)
        here = pl.ds(PAD + r, CHUNK)
        north_rows = pl.ds(PAD + r + 1, CHUNK)
        south_rows = pl.ds(PAD + r - 1, CHUNK)
        h = hd[l, e, here]
        north = h + hd[l, e, north_rows]
        south = h + hd[l, e, south_rows]
        above = h + hd[l, e + 1, here]
        below = wzs[l, e - 1, flat]
        east = h + near2[e, flat, 0:N]
        west = h + near2[e, flat, N : 2 * N]
        if r == 0:
            wys[l, e, 0:PAD] = jnp.broadcast_to(h[0:1], (PAD, N))
        wys[l, e, here] = north
        wzs[l, e, flat] = above
        wes[l, e, flat] = east
        wws[l, e, flat] = west
        total = ab[l, e, flat] + above + below + north + south + east + west
        scale = inside(e) / total
        inv[l, e, flat] = scale
        flow = (
            above * fl[l, e + 1, here]
            + below * fl[l, e - 1, here]
            + north * fl[l, e, north_rows]
            + south * fl[l, e, south_rows]
            + east * near[e, flat, 0:N]
            + west * near[e, flat, N : 2 * N]
        )
        tmp[l, e, here] = (spectra[l, 5] * lit[flat] + flow) * scale

    per_plane(1, EXT - 1, (fl, hd), first)

    def second(l, e, r):
        flat = pl.ds(r, CHUNK)
        here = pl.ds(PAD + r, CHUNK)
        scale = inv[l, e, flat]
        f = (spectra[l, 5] * lit[flat] + moved(tmp, l, e, r)) * scale
        fl[l, e, here] = f
        absorb = ab[l, e, flat]
        misfit = absorb * f - ms[l, e - (HF - HM), flat]
        ms[l, e - (HF - HM), flat] = misfit
        adj[l, e, here] = absorb * misfit * scale

    for copy in meas_copies:
        copy.wait()
    per_plane(2, EXT - 2, (tmp,), second)
    write = pltpu.make_async_copy(fl.at[:, pl.ds(HF, NP), whole], fluence, sem.at[0])
    write.start()
    for l in range(4):
        tmp[l, HF - 1] = jnp.zeros((N + 2 * PAD, N), F32)
        tmp[l, HF + NP] = jnp.zeros((N + 2 * PAD, N), F32)

    def third(l, e, r):
        flat = pl.ds(r, CHUNK)
        here = pl.ds(PAD + r, CHUNK)
        tmp[l, e, here] = (ab[l, e, flat] * ms[l, e - (HF - HM), flat] + moved(adj, l, e, r)) * inv[l, e, flat]

    per_plane(HF, HF + NP, (adj,), third)

    def couple(l, e, r):
        flat = pl.ds(r, CHUNK)
        here = pl.ds(PAD + r, CHUNK)
        north = pl.ds(PAD + r + 1, CHUNK)
        south = pl.ds(PAD + r - 1, CHUNK)
        h = hd[l, e, here]
        f = fl[l, e, here]
        a = tmp[l, e, here]
        total = (
            wes[l, e, flat] * (near[e, flat, 0:N] - f) * (near2[e, flat, 0:N] - a)
            + wws[l, e, flat] * (near[e, flat, N : 2 * N] - f) * (near2[e, flat, N : 2 * N] - a)
            + wys[l, e, here] * (fl[l, e, north] - f) * (tmp[l, e, north] - a)
            + wys[l, e, south] * (fl[l, e, south] - f) * (tmp[l, e, south] - a)
            + wzs[l, e, flat] * (fl[l, e + 1, here] - f) * (tmp[l, e + 1, here] - a)
            + wzs[l, e - 1, flat] * (fl[l, e - 1, here] - f) * (tmp[l, e - 1, here] - a)
        )
        ab[l, e, flat] = 12.0 * h * h * total

    per_plane(HF, HF + NP, (fl, tmp), couple)

    for coef, edge, high in ((coef_a, edge_a, 1 - odd), (coef_b, edge_b, odd)):
        e = HF + high * (NP - 1)
        beyond = e + 2 * high - 1
        face = e + high - 1
        for l in range(4):
            for c in range(N // CHUNK):
                here = pl.ds(PAD + c * CHUNK, CHUNK)
                to = pl.ds(c * CHUNK, CHUNK)
                h = hd[l, e, here]
                edge[l, to] = tmp[l, e, here]
                coef[l, to] = (
                    spectra[l, 4] * 12.0 * h * h * wzs[l, face, to] * (fl[l, beyond, here] - fl[l, e, here])
                )

    for code in range(8):
        rows = pl.ds(pl.multiple_of(PAD + (me ^ code) * ROWS, 8), ROWS)
        flat = pl.ds(pl.multiple_of((me ^ code) * ROWS, 8), ROWS)
        for plane in range(NP):
            e = plane + HF
            common = [fl[l, e, rows] * (ms[l, e - (HF - HM), flat] - tmp[l, e, rows]) for l in range(4)]
            paired = [ab[l, e, flat] for l in range(4)]
            for field in range(5):
                terms = common if field < 4 else paired
                value = spectra[0, field] * terms[0]
                for l in range(1, 4):
                    value = value + spectra[l, field] * terms[l]
                part, index = part_of(plane, field)
                slot = slot_of(part, code)
                if slot >= 4:
                    sends[part][slot - 4, index] = value
                else:
                    keeps[part][slot, index] = value
    write.wait()


def edge_kernel(where, coef_a, coef_b, edge_a, edge_b, send, keep):
    gz, me = where[0], where[1]
    there = jnp.where((gz > 0) & (gz < 31), 1.0, 0.0).astype(F32)
    for code in range(8):
        rows = pl.ds(pl.multiple_of((me ^ code) * ROWS, ROWS), ROWS)
        slot = slot_of(0, code)
        for side, (coef, edge) in enumerate(((coef_a, edge_a), (coef_b, edge_b))):
            value = coef[0, rows] * edge[0, rows]
            for l in range(1, 4):
                value = value + coef[l, rows] * edge[l, rows]
            if side:
                value = value * there
            if slot >= 4:
                send[slot - 4, side] = value
            else:
                keep[slot, side] = value


def squares_kernel(where, late_keep, late_recv, *refs):
    keeps, recvs, owns, sums = refs[:3], refs[3:6], refs[6:9], refs[9]
    odd = lax.rem(where[0], 2)
    total = [jnp.zeros((8, N), F32) for _ in range(5)]
    for plane in range(NP):
        for field in range(5):
            part, index = part_of(plane, field)
            value = keeps[part][0, index] + recvs[part][0, index]
            if field == 4 and plane in (0, NP - 1):
                side = 1 - odd if plane == 0 else odd
                value = value + (late_keep[0, side] + late_recv[0, side])
            owns[part][0, index] = value
            squared = value * value
            total[field] = total[field] + squared[:8] + squared[8:]
    lane = lax.broadcasted_iota(jnp.int32, (1, N), 1)
    row = jnp.zeros((1, N), F32)
    for field in range(5):
        whole = jnp.sum(jnp.sum(total[field], axis=0, keepdims=True), axis=1, keepdims=True)
        row = jnp.where(lane == field, whole, row)
    for target in range(32):
        sums[target] = row


def final_kernel(where, table, labels, *refs):
    pieces, (conc, scat, done, sem) = refs[:12], refs[12:]
    me = where[1]
    cells = 32 * NP * N * N
    extra = PARTS[0][1]
    total = pieces[0][0, extra] + pieces[1][0, extra]
    for i in range(2):
        total = total + pieces[2][i, extra]
    for i in range(4):
        total = total + pieces[3][i, extra]
    factor = -STEP / jnp.sqrt(total / cells + 1e-06)
    factors = [jnp.broadcast_to(factor[:, c : c + 1], (ROWS, N)) for c in range(5)]
    copies = []
    for plane in range(NP):
        for code in range(8):
            rows = pl.ds(pl.multiple_of((me ^ code) * ROWS, ROWS), ROWS)
            classes = labels[plane, rows]
            for field in range(5):
                part, index = part_of(plane, field)
                slot = slot_of(part, code)
                own, one, two, four = pieces[4 * part : 4 * part + 4]
                if slot == 0:
                    grad = own[0, index]
                elif slot == 1:
                    grad = one[0, index]
                elif slot < 4:
                    grad = two[slot - 2, index]
                else:
                    grad = four[slot - 4, index]
                coeff = pick(classes, [table[i, field] for i in range(8)])
                done[field, plane, rows] = coeff * jnp.exp(grad * factors[field])
        copies.append(pltpu.make_async_copy(done.at[0:4, plane], conc.at[:, plane], sem.at[plane, 0]))
        copies.append(pltpu.make_async_copy(done.at[4, plane], scat.at[plane], sem.at[plane, 1]))
        copies[-2].start()
        copies[-1].start()
    for copy in copies:
        copy.wait()


VMEM = pl.BlockSpec(memory_space=pltpu.VMEM)
SMEM = pl.BlockSpec(memory_space=pltpu.SMEM)
ANY = pl.BlockSpec(memory_space=pl.ANY)


def swap(x, code):
    return lax.ppermute(x, "wl", [(i, i ^ code) for i in range(8)])


ON_CHIP = [(i, i ^ 1) for i in range(32)]
OFF_CHIP = [(i, (i + 1 if i % 2 else i - 1) % 32) for i in range(32)]
AROUND = [(i, i - 7 if i % 8 == 7 else i + 7 if i % 8 == 0 else j) for i, j in OFF_CHIP]
ALONG = [(i, i + 8) for i in (0, 8, 16)] + [(i, i - 8) for i in (15, 23, 31)]


def beside(a, b):
    return lax.ppermute(a, "gz", ON_CHIP), lax.ppermute(b, "gz", OFF_CHIP)


def shards(labels, label_table, spectra, illumination, fluence_start, measured):
    where = jnp.stack([lax.axis_index("gz"), lax.axis_index("wl")]).astype(jnp.int32)
    odd = lax.rem(where[:1], 2)
    small = pltpu.CompilerParams(vmem_limit_bytes=12 * 2**20)

    def in_hbm(x):
        return pltpu.with_memory_space_constraint(x, pltpu.HBM)

    def in_vmem(x):
        return pltpu.with_memory_space_constraint(x, pltpu.VMEM)

    def pack(high, *planes):
        return pl.pallas_call(
            pack_kernel,
            out_shape=[jax.ShapeDtypeStruct((count, N, N), F32) for count in planes],
            in_specs=[SMEM] + [ANY] * 3,
            out_specs=[VMEM] * len(planes),
            scratch_shapes=[pltpu.VMEM((HF, N, N), jnp.int32), pltpu.SemaphoreType.DMA((9,))],
            compiler_params=small,
            name="pack",
        )(high, *map(in_hbm, (labels, fluence_start, measured)))

    bulk_b, extra_b = pack(odd, 4 * HF, 4 * HM + HF)
    (side_a,) = pack(1 - odd, 4 * HF + 4 * HM + HF)
    bulk_b = lax.ppermute(bulk_b, "gz", OFF_CHIP)
    straight_b = lax.ppermute(extra_b, "gz", AROUND)
    side_a = lax.ppermute(side_a, "gz", ON_CHIP)
    turned_b = lax.ppermute(straight_b, "gz", ALONG)
    side_a, bulk_b, straight_b, turned_b = map(in_vmem, (side_a, bulk_b, straight_b, turned_b))

    absorb_t = spectra[:, 0, None] * label_table[None, :, 0]
    for c in range(1, 4):
        absorb_t = absorb_t + spectra[:, c, None] * label_table[None, :, c]
    half_t = 0.5 / (3.0 * (absorb_t + spectra[:, 4, None] * label_table[None, :, 4]))

    sizes = [last - first for first, last in PARTS]
    field = pltpu.VMEM((4, EXT, N + 2 * PAD, N), F32)
    plane = jax.ShapeDtypeStruct((4, N, N), F32)
    fluence, coef_a, coef_b, edge_a, edge_b, *out = pl.pallas_call(
        solve_kernel,
        out_shape=[jax.ShapeDtypeStruct((4, NP, N, N), F32)]
        + [plane] * 4
        + [jax.ShapeDtypeStruct((4, size, ROWS, N), F32) for size in sizes for _ in range(2)],
        in_specs=[SMEM] * 4 + [ANY] + [VMEM] + [ANY] * 6,
        out_specs=[ANY] + [VMEM] * 10,
        scratch_shapes=[
            pltpu.VMEM((NP, N, N), jnp.int32),
            pltpu.VMEM((2 * HF, N, N), F32),
            pltpu.VMEM((N, N), F32),
            pltpu.VMEM((2 * N, 2 * N), jnp.bfloat16),
        ]
        + [pltpu.VMEM((EXT, N, 2 * N), F32)] * 2
        + [field] * 5
        + [pltpu.VMEM((4, EXT, N, N), F32)] * 5
        + [pltpu.VMEM((4, NP + 2 * HM, N, N), F32), pltpu.SemaphoreType.DMA((21,))],
        compiler_params=pltpu.CompilerParams(vmem_limit_bytes=52 * 2**20),
        name="solve",
    )(where, spectra, absorb_t, half_t, labels, illumination,
      *map(in_hbm, (fluence_start, measured)), side_a, bulk_b, straight_b, turned_b)
    sends = list(out[0::2])
    keeps = list(out[1::2])

    far_a, far_b = beside(edge_a, edge_b)
    for phase in range(2):
        recvs = [swap(sends[q], GENS[ORDERS[q][phase]]) for q in range(3)]
        half = keeps[0].shape[0] // 2
        sends = [keeps[q][half:] + recvs[q][half:] for q in range(3)]
        keeps = [keeps[q][:half] + recvs[q][:half] for q in range(3)]
        if phase == 0:
            far_a, far_b = lax.optimization_barrier((far_a, far_b, *sends))[:2]
    recvs = [swap(sends[q], GENS[ORDERS[q][2]]) for q in range(3)]

    late_send, late_keep = pl.pallas_call(
        edge_kernel,
        out_shape=[jax.ShapeDtypeStruct((4, 2, ROWS, N), F32)] * 2,
        in_specs=[SMEM] + [VMEM] * 4,
        out_specs=[VMEM] * 2,
        compiler_params=small,
        name="edge",
    )(where, coef_a, coef_b, far_a, far_b)
    for phase in range(2):
        late_recv = swap(late_send, GENS[ORDERS[0][phase]])
        half = late_keep.shape[0] // 2
        late_send = late_keep[half:] + late_recv[half:]
        late_keep = late_keep[:half] + late_recv[:half]
    late_recv = swap(late_send, GENS[ORDERS[0][2]])

    *owns, sums = pl.pallas_call(
        squares_kernel,
        out_shape=[jax.ShapeDtypeStruct((1, size, ROWS, N), F32) for size in sizes]
        + [jax.ShapeDtypeStruct((32, 1, N), F32)],
        in_specs=[SMEM] + [VMEM] * 8,
        out_specs=[VMEM] * 4,
        compiler_params=small,
        name="squares",
    )(where, late_keep, late_recv, *keeps, *recvs)

    steps = {q: [owns[q]] for q in (1, 2)}
    for phase in (2, 1, 0):
        for q in (1, 2):
            have = steps[q]
            mine = have[0] if len(have) == 1 else jnp.concatenate(have)
            have.append(swap(mine, GENS[ORDERS[q][phase]]))
    slab = jnp.sum(lax.all_to_all(sums, "gz", 0, 0), axis=0)
    steps[0] = [jnp.concatenate([owns[0], jnp.broadcast_to(slab[None, None], (1, 1, ROWS, N))], axis=1)]
    for phase in (2, 1, 0):
        have = steps[0]
        mine = have[0] if len(have) == 1 else jnp.concatenate(have)
        have.append(swap(mine, GENS[ORDERS[0][phase]]))
    pieces = steps[0] + steps[1] + steps[2]
    conc, scat = pl.pallas_call(
        final_kernel,
        out_shape=[jax.ShapeDtypeStruct((4, NP, N, N), F32), jax.ShapeDtypeStruct((NP, N, N), F32)],
        in_specs=[SMEM] * 2 + [VMEM] * 13,
        out_specs=[ANY] * 2,
        scratch_shapes=[pltpu.VMEM((5, NP, N, N), F32), pltpu.SemaphoreType.DMA((NP, 2))],
        compiler_params=pltpu.CompilerParams(vmem_limit_bytes=32 * 2**20),
        name="final",
    )(where, label_table, labels, *pieces)
    return fluence, conc, scat


def solution(mesh):
    in_specs = (
        P("gz", None, None),
        P(),
        P("wl", None),
        P(),
        P("wl", "gz", None, None),
        P("wl", "gz", None, None),
    )
    out_specs = (P("wl", "gz", None, None), P(None, "gz", None, None), P("gz", None, None))
    return jax.shard_map(shards, mesh=mesh, in_specs=in_specs, out_specs=out_specs, check_vma=False)
```

```python
import functools

import jax
import jax.numpy as jnp
from jax import lax
from jax.experimental import pallas as pl
from jax.experimental.pallas import tpu as pltpu
from jax.sharding import PartitionSpec as P

STEP = 0.3
HF = 3
HM = 1
NP = 8
EXT = NP + 2 * HF
N = 128
PAD = 8
CHUNK = 32
F32 = jnp.float32

GENS = (2, 6, 1)
ORDERS = ((0, 1, 2), (1, 2, 0), (2, 0, 1))
PARTS = ((0, 14), (14, 27), (27, 40))
ROWS = 16


def code_of(part, slot):
    order = ORDERS[part]
    bits = (slot >> 2 & 1, slot >> 1 & 1, slot & 1)
    code = 0
    for dim, bit in zip(order, bits):
        code ^= GENS[dim] * bit
    return code


def slot_of(part, code):
    return [code_of(part, slot) for slot in range(8)].index(code)


def part_of(plane, field):
    at = plane * 5 + field
    for part, (first, last) in enumerate(PARTS):
        if at < last:
            return part, at - first


def shifts():
    source = lax.broadcasted_iota(jnp.int32, (2 * N, 2 * N), 0)
    target = lax.broadcasted_iota(jnp.int32, (2 * N, 2 * N), 1)
    x = jnp.where(source >= N, source - N, source)
    ahead = (target < N) & (x == target + 1)
    behind = (target >= N) & (x == target - N - 1)
    return jnp.where(ahead | behind, 1.0, 0.0).astype(jnp.bfloat16)


def two_terms(v):
    high = v.astype(jnp.bfloat16)
    low = (v - high.astype(F32)).astype(jnp.bfloat16)
    return jnp.concatenate([high, low], axis=1)


def pick(classes, entries):
    bit0 = (classes & 1) != 0
    bit1 = (classes & 2) != 0
    bit2 = (classes & 4) != 0
    low = [jnp.where(bit0, entries[2 * i + 1], entries[2 * i]) for i in range(4)]
    mid = [jnp.where(bit1, low[2 * i + 1], low[2 * i]) for i in range(2)]
    return jnp.where(bit2, mid[1], mid[0])


def pack_kernel(high, labels, start, meas, *rest):
    *outs, ints, sem = rest
    bulk, extra = outs[0], outs[-1]
    at = 4 * HF if len(outs) == 1 else 0
    flip = high[0]
    copies = [pltpu.make_async_copy(labels.at[pl.ds(flip * (NP - HF), HF)], ints, sem.at[8])]
    for l in range(4):
        copies.append(
            pltpu.make_async_copy(start.at[l, pl.ds(flip * (NP - HF), HF)], bulk.at[pl.ds(l * HF, HF)], sem.at[l])
        )
        copies.append(
            pltpu.make_async_copy(
                meas.at[l, pl.ds(flip * (NP - HM), HM)], extra.at[pl.ds(at + l * HM, HM)], sem.at[4 + l]
            )
        )
    for copy in copies:
        copy.start()
    for copy in copies:
        copy.wait()
    extra[at + 4 * HM : at + 4 * HM + HF] = ints[...].astype(F32)


def stages(where, spectra, absorb_t, half_t, lit, step, near, near2, state):
    fl, hd, wys, tmp, adj, ab, wes, wws, wzs, inv, ms = state
    gz = where[0]
    pad = jnp.zeros((PAD, N), F32)

    def inside(e):
        z = gz * NP + e - HF
        return jnp.where((z >= 0) & (z < 32 * NP), 1.0, 0.0).astype(F32)

    def clear(e, _):
        for l in range(4):
            for field in (fl, tmp, adj, hd):
                field[l, e, 0:PAD] = pad
                field[l, e, PAD + N : 2 * PAD + N] = pad
        return 0

    def optics(classes, e, r):
        there = inside(e)
        flat = pl.ds(r, CHUNK)
        rows = pl.ds(PAD + r, CHUNK)
        for l in range(4):
            ab[l, e, flat] = pick(classes, [absorb_t[l, i] for i in range(8)])
            hd[l, e, rows] = pick(classes, [half_t[l, i] * there for i in range(8)])

    def per_plane(ranges, fields, body):
        def spread(to, field, l):
            parts = [field[l, a:b, PAD : PAD + N].reshape((b - a) * N, N) for a, b in ranges]
            rows = parts[0] if len(parts) == 1 else jnp.concatenate(parts)
            both = jnp.dot(two_terms(rows), step[...], preferred_element_type=F32)
            at = 0
            for a, b in ranges:
                to[a:b] = both[at : at + (b - a) * N].reshape(b - a, N, 2 * N)
                at += (b - a) * N

        def outerloop(l, _):
            for to, field in zip((near, near2), fields):
                spread(to, field, l)

            def innerloop(e, _):
                for c in range(N // CHUNK):
                    body(l, e, c * CHUNK)
                return 0

            for a, b in ranges:
                lax.fori_loop(a, b, innerloop, 0)
            return 0

        lax.fori_loop(0, 4, outerloop, 0)

    def face(e):
        for l in range(4):
            for c in range(N // CHUNK):
                here = pl.ds(PAD + c * CHUNK, CHUNK)
                wzs[l, e, pl.ds(c * CHUNK, CHUNK)] = hd[l, e, here] + hd[l, e + 1, here]

    def moved(field, l, e, r):
        flat = pl.ds(r, CHUNK)
        here = pl.ds(PAD + r, CHUNK)
        north = pl.ds(PAD + r + 1, CHUNK)
        south = pl.ds(PAD + r - 1, CHUNK)
        return (
            wzs[l, e, flat] * field[l, e + 1, here]
            + wzs[l, e - 1, flat] * field[l, e - 1, here]
            + wys[l, e, here] * field[l, e, north]
            + wys[l, e, south] * field[l, e, south]
            + wes[l, e, flat] * near[e, flat, 0:N]
            + wws[l, e, flat] * near[e, flat, N : 2 * N]
        )

    def first(l, e, r):
        flat = pl.ds(r, CHUNK)
        here = pl.ds(PAD + r, CHUNK)
        north_rows = pl.ds(PAD + r + 1, CHUNK)
        south_rows = pl.ds(PAD + r - 1, CHUNK)
        h = hd[l, e, here]
        north = h + hd[l, e, north_rows]
        south = h + hd[l, e, south_rows]
        above = h + hd[l, e + 1, here]
        below = wzs[l, e - 1, flat]
        east = h + near2[e, flat, 0:N]
        west = h + near2[e, flat, N : 2 * N]
        if r == 0:
            wys[l, e, 0:PAD] = jnp.broadcast_to(h[0:1], (PAD, N))
        wys[l, e, here] = north
        wzs[l, e, flat] = above
        wes[l, e, flat] = east
        wws[l, e, flat] = west
        total = ab[l, e, flat] + above + below + north + south + east + west
        scale = inside(e) / total
        inv[l, e, flat] = scale
        flow = (
            above * fl[l, e + 1, here]
            + below * fl[l, e - 1, here]
            + north * fl[l, e, north_rows]
            + south * fl[l, e, south_rows]
            + east * near[e, flat, 0:N]
            + west * near[e, flat, N : 2 * N]
        )
        tmp[l, e, here] = (spectra[l, 5] * lit[flat] + flow) * scale

    def second(l, e, r):
        flat = pl.ds(r, CHUNK)
        here = pl.ds(PAD + r, CHUNK)
        scale = inv[l, e, flat]
        f = (spectra[l, 5] * lit[flat] + moved(tmp, l, e, r)) * scale
        fl[l, e, here] = f
        absorb = ab[l, e, flat]
        misfit = absorb * f - ms[l, e - (HF - HM), flat]
        ms[l, e - (HF - HM), flat] = misfit
        adj[l, e, here] = absorb * misfit * scale

    def third(l, e, r):
        flat = pl.ds(r, CHUNK)
        here = pl.ds(PAD + r, CHUNK)
        tmp[l, e, here] = (ab[l, e, flat] * ms[l, e - (HF - HM), flat] + moved(adj, l, e, r)) * inv[l, e, flat]

    def couple(l, e, r):
        flat = pl.ds(r, CHUNK)
        here = pl.ds(PAD + r, CHUNK)
        north = pl.ds(PAD + r + 1, CHUNK)
        south = pl.ds(PAD + r - 1, CHUNK)
        h = hd[l, e, here]
        f = fl[l, e, here]
        a = tmp[l, e, here]
        total = (
            wes[l, e, flat] * (near[e, flat, 0:N] - f) * (near2[e, flat, 0:N] - a)
            + wws[l, e, flat] * (near[e, flat, N : 2 * N] - f) * (near2[e, flat, N : 2 * N] - a)
            + wys[l, e, here] * (fl[l, e, north] - f) * (tmp[l, e, north] - a)
            + wys[l, e, south] * (fl[l, e, south] - f) * (tmp[l, e, south] - a)
            + wzs[l, e, flat] * (fl[l, e + 1, here] - f) * (tmp[l, e + 1, here] - a)
            + wzs[l, e - 1, flat] * (fl[l, e - 1, here] - f) * (tmp[l, e - 1, here] - a)
        )
        ab[l, e, flat] = 12.0 * h * h * total

    return inside, clear, optics, per_plane, face, first, second, third, couple


def inner_kernel(where, spectra, absorb_t, half_t, labels, illum, start, meas, *rest):
    state, (own, lit, step, near, near2, sem) = rest[:11], rest[11:]
    fl, hd, wys, tmp, adj, ab, wes, wws, wzs, inv, ms = state
    _, clear, optics, per_plane, face, first, second, third, _ = stages(
        where, spectra, absorb_t, half_t, lit, step, near, near2, state
    )
    copies = [
        pltpu.make_async_copy(labels, own, sem.at[0]),
        pltpu.make_async_copy(start, fl.at[:, pl.ds(HF, NP), pl.ds(PAD, N)], sem.at[1]),
        pltpu.make_async_copy(meas, ms.at[:, pl.ds(HM, NP)], sem.at[2]),
    ]
    for copy in copies:
        copy.start()
    lit[...] = illum[...].astype(F32)
    step[...] = shifts()
    lax.fori_loop(0, EXT, clear, 0)

    def optics_own(p, _):
        for c in range(N // CHUNK):
            optics(own[p, pl.ds(c * CHUNK, CHUNK)], p + HF, c * CHUNK)
        return 0

    copies[0].wait()
    lax.fori_loop(0, NP, optics_own, 0)
    face(HF)
    copies[1].wait()
    per_plane(((HF + 1, HF + NP - 1),), (fl, hd), first)
    copies[2].wait()
    per_plane(((HF + 2, HF + NP - 2),), (tmp,), second)
    per_plane(((HF + 3, HF + NP - 3),), (adj,), third)


def solve_kernel(
    where, spectra, absorb_t, half_t, illum, side_a, bulk_b, straight_b, turned_b, *rest,
):
    fluence, coef_a, coef_b, edge_a, edge_b, *rest = rest[11:]
    outs, state = rest[:6], rest[6:17]
    shared, lit, step, near, near2, sem = rest[17:]
    fl, hd, wys, tmp, adj, ab, wes, wws, wzs, inv, ms = state
    sends, keeps = outs[0::2], outs[1::2]
    inside, _, optics, per_plane, face, first, second, third, couple = stages(
        where, spectra, absorb_t, half_t, lit, step, near, near2, state
    )
    gz = where[0]
    me = where[1]
    odd = lax.rem(gz, 2)
    whole = pl.ds(PAD, N)

    def extras(side, at, high, number):
        first = 3 + 5 * number
        return [
            pltpu.make_async_copy(
                side.at[pl.ds(at + 4 * HM, HF)], shared.at[pl.ds(high * HF, HF)], sem.at[first]
            )
        ] + [
            pltpu.make_async_copy(
                side.at[pl.ds(at + l * HM, HM)], ms.at[l, pl.ds(high * (HM + NP), HM)], sem.at[first + 1 + l]
            )
            for l in range(4)
        ]

    extras_a = extras(side_a, 4 * HF, 1 - odd, 0)
    extras_b = extras(straight_b, 0, odd, 1)
    label_copies = [extras_a[0], extras_b[0]]
    meas_copies = extras_a[1:] + extras_b[1:]
    fluence_copies = [
        pltpu.make_async_copy(
            side.at[pl.ds(l * HF, HF)],
            fl.at[l, pl.ds(high * (HF + NP), HF), whole],
            sem.at[13 + 4 * number + l],
        )
        for number, (side, high) in enumerate(((side_a, 1 - odd), (bulk_b, odd)))
        for l in range(4)
    ]
    turned = (lax.rem(gz, 8) == 0) | (lax.rem(gz, 8) == 7)
    extras_a[0].start()

    @pl.when(turned)
    def _():
        for copy in extras(turned_b, 0, odd, 1):
            copy.start()

    @pl.when(jnp.logical_not(turned))
    def _():
        for copy in extras_b:
            copy.start()

    for copy in fluence_copies + extras_a[1:]:
        copy.start()

    lit[...] = illum[...].astype(F32)
    step[...] = shifts()

    def optics_shared(p, _):
        e = p + jnp.where(p < HF, 0, NP)
        for c in range(N // CHUNK):
            classes = shared[p, pl.ds(c * CHUNK, CHUNK)].astype(jnp.int32)
            optics(classes, e, c * CHUNK)
        return 0

    for copy in label_copies:
        copy.wait()
    lax.fori_loop(0, 2 * HF, optics_shared, 0)
    for copy in fluence_copies:
        copy.wait()

    @pl.when(gz == 0)
    def _():
        fl[:, HF - 1] = jnp.zeros((4, N + 2 * PAD, N), F32)

    @pl.when(gz == 31)
    def _():
        fl[:, HF + NP] = jnp.zeros((4, N + 2 * PAD, N), F32)

    face(0)
    last = HF + NP
    per_plane(((1, HF + 1), (last - 1, EXT - 1)), (fl, hd), first)
    for copy in meas_copies:
        copy.wait()
    per_plane(((2, HF + 2), (last - 2, EXT - 2)), (tmp,), second)
    write = pltpu.make_async_copy(fl.at[:, pl.ds(HF, NP), whole], fluence, sem.at[0])
    write.start()
    for l in range(4):
        tmp[l, HF - 1] = jnp.zeros((N + 2 * PAD, N), F32)
        tmp[l, last] = jnp.zeros((N + 2 * PAD, N), F32)
    per_plane(((HF, HF + 3), (last - 3, last)), (adj,), third)
    per_plane(((HF, last),), (fl, tmp), couple)

    for coef, edge, high in ((coef_a, edge_a, 1 - odd), (coef_b, edge_b, odd)):
        e = HF + high * (NP - 1)
        beyond = e + 2 * high - 1
        face = e + high - 1
        for l in range(4):
            for c in range(N // CHUNK):
                here = pl.ds(PAD + c * CHUNK, CHUNK)
                to = pl.ds(c * CHUNK, CHUNK)
                h = hd[l, e, here]
                edge[l, to] = tmp[l, e, here]
                coef[l, to] = (
                    spectra[l, 4] * 12.0 * h * h * wzs[l, face, to] * (fl[l, beyond, here] - fl[l, e, here])
                )

    for code in range(8):
        rows = pl.ds(pl.multiple_of(PAD + (me ^ code) * ROWS, 8), ROWS)
        flat = pl.ds(pl.multiple_of((me ^ code) * ROWS, 8), ROWS)
        for plane in range(NP):
            e = plane + HF
            common = [fl[l, e, rows] * (ms[l, e - (HF - HM), flat] - tmp[l, e, rows]) for l in range(4)]
            paired = [ab[l, e, flat] for l in range(4)]
            for field in range(5):
                terms = common if field < 4 else paired
                value = spectra[0, field] * terms[0]
                for l in range(1, 4):
                    value = value + spectra[l, field] * terms[l]
                part, index = part_of(plane, field)
                slot = slot_of(part, code)
                if slot >= 4:
                    sends[part][slot - 4, index] = value
                else:
                    keeps[part][slot, index] = value
    write.wait()


def edge_kernel(where, coef_a, coef_b, edge_a, edge_b, send, keep):
    gz, me = where[0], where[1]
    there = jnp.where((gz > 0) & (gz < 31), 1.0, 0.0).astype(F32)
    for code in range(8):
        rows = pl.ds(pl.multiple_of((me ^ code) * ROWS, ROWS), ROWS)
        slot = slot_of(0, code)
        for side, (coef, edge) in enumerate(((coef_a, edge_a), (coef_b, edge_b))):
            value = coef[0, rows] * edge[0, rows]
            for l in range(1, 4):
                value = value + coef[l, rows] * edge[l, rows]
            if side:
                value = value * there
            if slot >= 4:
                send[slot - 4, side] = value
            else:
                keep[slot, side] = value


def squares_kernel(where, late_keep, late_recv, *refs):
    keeps, recvs, owns, sums = refs[:3], refs[3:6], refs[6:9], refs[9]
    odd = lax.rem(where[0], 2)
    total = [jnp.zeros((8, N), F32) for _ in range(5)]
    for plane in range(NP):
        for field in range(5):
            part, index = part_of(plane, field)
            value = keeps[part][0, index] + recvs[part][0, index]
            if field == 4 and plane in (0, NP - 1):
                side = 1 - odd if plane == 0 else odd
                value = value + (late_keep[0, side] + late_recv[0, side])
            owns[part][0, index] = value
            squared = value * value
            total[field] = total[field] + squared[:8] + squared[8:]
    lane = lax.broadcasted_iota(jnp.int32, (1, N), 1)
    row = jnp.zeros((1, N), F32)
    for field in range(5):
        whole = jnp.sum(jnp.sum(total[field], axis=0, keepdims=True), axis=1, keepdims=True)
        row = jnp.where(lane == field, whole, row)
    for target in range(32):
        sums[target] = row


def final_kernel(where, table, labels, *refs):
    pieces, (conc, scat, done, sem) = refs[:12], refs[12:]
    me = where[1]
    cells = 32 * NP * N * N
    extra = PARTS[0][1]
    total = pieces[0][0, extra] + pieces[1][0, extra]
    for i in range(2):
        total = total + pieces[2][i, extra]
    for i in range(4):
        total = total + pieces[3][i, extra]
    factor = -STEP / jnp.sqrt(total / cells + 1e-06)
    factors = [jnp.broadcast_to(factor[:, c : c + 1], (ROWS, N)) for c in range(5)]
    copies = []
    for plane in range(NP):
        for code in range(8):
            rows = pl.ds(pl.multiple_of((me ^ code) * ROWS, ROWS), ROWS)
            classes = labels[plane, rows]
            for field in range(5):
                part, index = part_of(plane, field)
                slot = slot_of(part, code)
                own, one, two, four = pieces[4 * part : 4 * part + 4]
                if slot == 0:
                    grad = own[0, index]
                elif slot == 1:
                    grad = one[0, index]
                elif slot < 4:
                    grad = two[slot - 2, index]
                else:
                    grad = four[slot - 4, index]
                coeff = pick(classes, [table[i, field] for i in range(8)])
                done[field, plane, rows] = coeff * jnp.exp(grad * factors[field])
        copies.append(pltpu.make_async_copy(done.at[0:4, plane], conc.at[:, plane], sem.at[plane, 0]))
        copies.append(pltpu.make_async_copy(done.at[4, plane], scat.at[plane], sem.at[plane, 1]))
        copies[-2].start()
        copies[-1].start()
    for copy in copies:
        copy.wait()


VMEM = pl.BlockSpec(memory_space=pltpu.VMEM)
SMEM = pl.BlockSpec(memory_space=pltpu.SMEM)
ANY = pl.BlockSpec(memory_space=pl.ANY)


def swap(x, code):
    return lax.ppermute(x, "wl", [(i, i ^ code) for i in range(8)])


ON_CHIP = [(i, i ^ 1) for i in range(32)]
OFF_CHIP = [(i, (i + 1 if i % 2 else i - 1) % 32) for i in range(32)]
AROUND = [(i, i - 7 if i % 8 == 7 else i + 7 if i % 8 == 0 else j) for i, j in OFF_CHIP]
ALONG = [(i, i + 8) for i in (0, 8, 16)] + [(i, i - 8) for i in (15, 23, 31)]


def beside(a, b):
    return lax.ppermute(a, "gz", ON_CHIP), lax.ppermute(b, "gz", OFF_CHIP)


def shards(labels, label_table, spectra, illumination, fluence_start, measured):
    where = jnp.stack([lax.axis_index("gz"), lax.axis_index("wl")]).astype(jnp.int32)
    odd = lax.rem(where[:1], 2)
    small = pltpu.CompilerParams(vmem_limit_bytes=12 * 2**20)

    def in_hbm(x):
        return pltpu.with_memory_space_constraint(x, pltpu.HBM)

    def in_vmem(x):
        return pltpu.with_memory_space_constraint(x, pltpu.VMEM)

    def pack(high, *planes):
        return pl.pallas_call(
            pack_kernel,
            out_shape=[jax.ShapeDtypeStruct((count, N, N), F32) for count in planes],
            in_specs=[SMEM] + [ANY] * 3,
            out_specs=[VMEM] * len(planes),
            scratch_shapes=[pltpu.VMEM((HF, N, N), jnp.int32), pltpu.SemaphoreType.DMA((9,))],
            compiler_params=small,
            name="pack",
        )(high, *map(in_hbm, (labels, fluence_start, measured)))

    bulk_b, extra_b = pack(odd, 4 * HF, 4 * HM + HF)
    (side_a,) = pack(1 - odd, 4 * HF + 4 * HM + HF)
    bulk_b = lax.ppermute(bulk_b, "gz", OFF_CHIP)
    straight_b = lax.ppermute(extra_b, "gz", AROUND)
    side_a = lax.ppermute(side_a, "gz", ON_CHIP)
    turned_b = lax.ppermute(straight_b, "gz", ALONG)
    side_a, bulk_b, straight_b, turned_b = map(in_vmem, (side_a, bulk_b, straight_b, turned_b))

    absorb_t = spectra[:, 0, None] * label_table[None, :, 0]
    for c in range(1, 4):
        absorb_t = absorb_t + spectra[:, c, None] * label_table[None, :, c]
    half_t = 0.5 / (3.0 * (absorb_t + spectra[:, 4, None] * label_table[None, :, 4]))

    sizes = [last - first for first, last in PARTS]
    plane = jax.ShapeDtypeStruct((4, N, N), F32)
    held = (
        [pltpu.VMEM((4, EXT, N + 2 * PAD, N), F32)] * 5
        + [pltpu.VMEM((4, EXT, N, N), F32)] * 5
        + [pltpu.VMEM((4, NP + 2 * HM, N, N), F32)]
    )
    work = [
        pltpu.VMEM((N, N), F32),
        pltpu.VMEM((2 * N, 2 * N), jnp.bfloat16),
        pltpu.VMEM((EXT, N, 2 * N), F32),
        pltpu.VMEM((EXT, N, 2 * N), F32),
    ]
    state = pl.pallas_call(
        inner_kernel,
        out_shape=held,
        in_specs=[SMEM] * 4 + [ANY] + [VMEM] + [ANY] * 2,
        out_specs=[VMEM] * 11,
        scratch_shapes=[pltpu.VMEM((NP, N, N), jnp.int32)] + work + [pltpu.SemaphoreType.DMA((3,))],
        compiler_params=small,
        name="inner",
    )(where, spectra, absorb_t, half_t, in_hbm(labels), illumination, *map(in_hbm, (fluence_start, measured)))
    fluence, coef_a, coef_b, edge_a, edge_b, *out = pl.pallas_call(
        solve_kernel,
        out_shape=[jax.ShapeDtypeStruct((4, NP, N, N), F32)]
        + [plane] * 4
        + [jax.ShapeDtypeStruct((4, size, ROWS, N), F32) for size in sizes for _ in range(2)]
        + held,
        in_specs=[SMEM] * 4 + [VMEM] + [ANY] * 4 + [VMEM] * 11,
        out_specs=[ANY] + [VMEM] * 21,
        input_output_aliases={9 + i: 11 + i for i in range(11)},
        scratch_shapes=[pltpu.VMEM((2 * HF, N, N), F32)] + work + [pltpu.SemaphoreType.DMA((21,))],
        compiler_params=small,
        name="solve",
    )(where, spectra, absorb_t, half_t, illumination, side_a, bulk_b, straight_b, turned_b, *map(in_vmem, state))
    out = out[:6]
    sends = list(out[0::2])
    keeps = list(out[1::2])

    far_a, far_b = beside(edge_a, edge_b)
    for phase in range(2):
        recvs = [swap(sends[q], GENS[ORDERS[q][phase]]) for q in range(3)]
        half = keeps[0].shape[0] // 2
        sends = [keeps[q][half:] + recvs[q][half:] for q in range(3)]
        keeps = [keeps[q][:half] + recvs[q][:half] for q in range(3)]
        if phase == 0:
            far_a, far_b = lax.optimization_barrier((far_a, far_b, *sends))[:2]
    recvs = [swap(sends[q], GENS[ORDERS[q][2]]) for q in range(3)]

    late_send, late_keep = pl.pallas_call(
        edge_kernel,
        out_shape=[jax.ShapeDtypeStruct((4, 2, ROWS, N), F32)] * 2,
        in_specs=[SMEM] + [VMEM] * 4,
        out_specs=[VMEM] * 2,
        compiler_params=small,
        name="edge",
    )(where, coef_a, coef_b, far_a, far_b)
    for phase in range(2):
        late_recv = swap(late_send, GENS[ORDERS[0][phase]])
        half = late_keep.shape[0] // 2
        late_send = late_keep[half:] + late_recv[half:]
        late_keep = late_keep[:half] + late_recv[:half]
    late_recv = swap(late_send, GENS[ORDERS[0][2]])

    *owns, sums = pl.pallas_call(
        squares_kernel,
        out_shape=[jax.ShapeDtypeStruct((1, size, ROWS, N), F32) for size in sizes]
        + [jax.ShapeDtypeStruct((32, 1, N), F32)],
        in_specs=[SMEM] + [VMEM] * 8,
        out_specs=[VMEM] * 4,
        compiler_params=small,
        name="squares",
    )(where, late_keep, late_recv, *keeps, *recvs)

    steps = {q: [owns[q]] for q in (1, 2)}
    for phase in (2, 1, 0):
        for q in (1, 2):
            have = steps[q]
            mine = have[0] if len(have) == 1 else jnp.concatenate(have)
            have.append(swap(mine, GENS[ORDERS[q][phase]]))
    slab = jnp.sum(lax.all_to_all(sums, "gz", 0, 0), axis=0)
    steps[0] = [jnp.concatenate([owns[0], jnp.broadcast_to(slab[None, None], (1, 1, ROWS, N))], axis=1)]
    for phase in (2, 1, 0):
        have = steps[0]
        mine = have[0] if len(have) == 1 else jnp.concatenate(have)
        have.append(swap(mine, GENS[ORDERS[0][phase]]))
    pieces = steps[0] + steps[1] + steps[2]
    conc, scat = pl.pallas_call(
        final_kernel,
        out_shape=[jax.ShapeDtypeStruct((4, NP, N, N), F32), jax.ShapeDtypeStruct((NP, N, N), F32)],
        in_specs=[SMEM] * 2 + [VMEM] * 13,
        out_specs=[ANY] * 2,
        scratch_shapes=[pltpu.VMEM((5, NP, N, N), F32), pltpu.SemaphoreType.DMA((NP, 2))],
        compiler_params=pltpu.CompilerParams(vmem_limit_bytes=32 * 2**20),
        name="final",
    )(where, label_table, labels, *pieces)
    return fluence, conc, scat


def solution(mesh):
    in_specs = (
        P("gz", None, None),
        P(),
        P("wl", None),
        P(),
        P("wl", "gz", None, None),
        P("wl", "gz", None, None),
    )
    out_specs = (P("wl", "gz", None, None), P(None, "gz", None, None), P("gz", None, None))
    return jax.shard_map(shards, mesh=mesh, in_specs=in_specs, out_specs=out_specs, check_vma=False)
```

```python
import functools

import jax
import jax.numpy as jnp
from jax import lax
from jax.experimental import pallas as pl
from jax.experimental.pallas import tpu as pltpu
from jax.sharding import PartitionSpec as P

STEP = 0.3
HF = 3
HM = 1
NP = 8
EXT = NP + 2 * HF
TOTAL = 4 * (HF + HM) + HF
BULK = 4 * HF + 2 * HM
N = 128
PAD = 8
CHUNK = 32
F32 = jnp.float32

GENS = (2, 6, 1)
ORDERS = ((0, 1, 2), (1, 2, 0), (2, 0, 1))
PARTS = ((0, 14), (14, 27), (27, 40))
ROWS = 16


def code_of(part, slot):
    order = ORDERS[part]
    bits = (slot >> 2 & 1, slot >> 1 & 1, slot & 1)
    code = 0
    for dim, bit in zip(order, bits):
        code ^= GENS[dim] * bit
    return code


def slot_of(part, code):
    return [code_of(part, slot) for slot in range(8)].index(code)


def part_of(plane, field):
    at = plane * 5 + field
    for part, (first, last) in enumerate(PARTS):
        if at < last:
            return part, at - first


def shifts():
    source = lax.broadcasted_iota(jnp.int32, (2 * N, 2 * N), 0)
    target = lax.broadcasted_iota(jnp.int32, (2 * N, 2 * N), 1)
    x = jnp.where(source >= N, source - N, source)
    ahead = (target < N) & (x == target + 1)
    behind = (target >= N) & (x == target - N - 1)
    return jnp.where(ahead | behind, 1.0, 0.0).astype(jnp.bfloat16)


def two_terms(v):
    high = v.astype(jnp.bfloat16)
    low = (v - high.astype(F32)).astype(jnp.bfloat16)
    return jnp.concatenate([high, low], axis=1)


def pick(classes, entries):
    bit0 = (classes & 1) != 0
    bit1 = (classes & 2) != 0
    bit2 = (classes & 4) != 0
    low = [jnp.where(bit0, entries[2 * i + 1], entries[2 * i]) for i in range(4)]
    mid = [jnp.where(bit1, low[2 * i + 1], low[2 * i]) for i in range(2)]
    return jnp.where(bit2, mid[1], mid[0])


def pack_kernel(where, labels, start, meas, bulk_b, extra_b, side_a, ints, sem):
    odd = lax.rem(where[0], 2)
    copies = []
    for side, flip in enumerate((odd, 1 - odd)):

        def place(at, count):
            if side == 1:
                return side_a.at[pl.ds(at, count)]
            return bulk_b.at[pl.ds(at, count)] if at < BULK else extra_b.at[pl.ds(at - BULK, count)]

        copies.append(
            pltpu.make_async_copy(labels.at[pl.ds(flip * (NP - HF), HF)], ints.at[side], sem.at[side, 8])
        )
        for l in range(4):
            copies.append(
                pltpu.make_async_copy(
                    start.at[l, pl.ds(flip * (NP - HF), HF)], place(l * HF, HF), sem.at[side, l]
                )
            )
            copies.append(
                pltpu.make_async_copy(
                    meas.at[l, pl.ds(flip * (NP - HM), HM)], place(4 * HF + l * HM, HM), sem.at[side, 4 + l]
                )
            )
    for copy in copies:
        copy.start()
    for copy in copies:
        copy.wait()
    extra_b[TOTAL - HF - BULK : TOTAL - BULK] = ints[0].astype(F32)
    side_a[TOTAL - HF : TOTAL] = ints[1].astype(F32)


def stages(where, spectra, absorb_t, half_t, lit, step, near, near2, state):
    fl, hd, wys, tmp, adj, ab, wes, wws, wzs, inv, ms = state
    gz = where[0]
    pad = jnp.zeros((PAD, N), F32)

    def inside(e):
        z = gz * NP + e - HF
        return jnp.where((z >= 0) & (z < 32 * NP), 1.0, 0.0).astype(F32)

    def clear(e, _):
        for l in range(4):
            for field in (fl, tmp, adj, hd):
                field[l, e, 0:PAD] = pad
                field[l, e, PAD + N : 2 * PAD + N] = pad
        return 0

    def optics(classes, e, r):
        there = inside(e)
        flat = pl.ds(r, CHUNK)
        rows = pl.ds(PAD + r, CHUNK)
        for l in range(4):
            ab[l, e, flat] = pick(classes, [absorb_t[l, i] for i in range(8)])
            hd[l, e, rows] = pick(classes, [half_t[l, i] * there for i in range(8)])

    def per_plane(ranges, fields, body):
        def spread(to, field, l):
            parts = [field[l, a:b, PAD : PAD + N].reshape((b - a) * N, N) for a, b in ranges]
            rows = parts[0] if len(parts) == 1 else jnp.concatenate(parts)
            both = jnp.dot(two_terms(rows), step[...], preferred_element_type=F32)
            at = 0
            for a, b in ranges:
                to[a:b] = both[at : at + (b - a) * N].reshape(b - a, N, 2 * N)
                at += (b - a) * N

        def outerloop(l, _):
            for to, field in zip((near, near2), fields):
                spread(to, field, l)

            def innerloop(e, _):
                for c in range(N // CHUNK):
                    body(l, e, c * CHUNK)
                return 0

            for a, b in ranges:
                lax.fori_loop(a, b, innerloop, 0)
            return 0

        lax.fori_loop(0, 4, outerloop, 0)

    def face(e):
        for l in range(4):
            for c in range(N // CHUNK):
                here = pl.ds(PAD + c * CHUNK, CHUNK)
                wzs[l, e, pl.ds(c * CHUNK, CHUNK)] = hd[l, e, here] + hd[l, e + 1, here]

    def moved(field, l, e, r):
        flat = pl.ds(r, CHUNK)
        here = pl.ds(PAD + r, CHUNK)
        north = pl.ds(PAD + r + 1, CHUNK)
        south = pl.ds(PAD + r - 1, CHUNK)
        return (
            wzs[l, e, flat] * field[l, e + 1, here]
            + wzs[l, e - 1, flat] * field[l, e - 1, here]
            + wys[l, e, here] * field[l, e, north]
            + wys[l, e, south] * field[l, e, south]
            + wes[l, e, flat] * near[e, flat, 0:N]
            + wws[l, e, flat] * near[e, flat, N : 2 * N]
        )

    def first(l, e, r):
        flat = pl.ds(r, CHUNK)
        here = pl.ds(PAD + r, CHUNK)
        north_rows = pl.ds(PAD + r + 1, CHUNK)
        south_rows = pl.ds(PAD + r - 1, CHUNK)
        h = hd[l, e, here]
        north = h + hd[l, e, north_rows]
        south = h + hd[l, e, south_rows]
        above = h + hd[l, e + 1, here]
        below = wzs[l, e - 1, flat]
        east = h + near2[e, flat, 0:N]
        west = h + near2[e, flat, N : 2 * N]
        if r == 0:
            wys[l, e, 0:PAD] = jnp.broadcast_to(h[0:1], (PAD, N))
        wys[l, e, here] = north
        wzs[l, e, flat] = above
        wes[l, e, flat] = east
        wws[l, e, flat] = west
        total = ab[l, e, flat] + above + below + north + south + east + west
        scale = inside(e) / total
        inv[l, e, flat] = scale
        flow = (
            above * fl[l, e + 1, here]
            + below * fl[l, e - 1, here]
            + north * fl[l, e, north_rows]
            + south * fl[l, e, south_rows]
            + east * near[e, flat, 0:N]
            + west * near[e, flat, N : 2 * N]
        )
        tmp[l, e, here] = (spectra[l, 5] * lit[flat] + flow) * scale

    def second(l, e, r):
        flat = pl.ds(r, CHUNK)
        here = pl.ds(PAD + r, CHUNK)
        scale = inv[l, e, flat]
        f = (spectra[l, 5] * lit[flat] + moved(tmp, l, e, r)) * scale
        fl[l, e, here] = f
        absorb = ab[l, e, flat]
        misfit = absorb * f - ms[l, e - (HF - HM), flat]
        ms[l, e - (HF - HM), flat] = misfit
        adj[l, e, here] = absorb * misfit * scale

    def third(l, e, r):
        flat = pl.ds(r, CHUNK)
        here = pl.ds(PAD + r, CHUNK)
        tmp[l, e, here] = (ab[l, e, flat] * ms[l, e - (HF - HM), flat] + moved(adj, l, e, r)) * inv[l, e, flat]

    def couple(l, e, r):
        flat = pl.ds(r, CHUNK)
        here = pl.ds(PAD + r, CHUNK)
        north = pl.ds(PAD + r + 1, CHUNK)
        south = pl.ds(PAD + r - 1, CHUNK)
        h = hd[l, e, here]
        f = fl[l, e, here]
        a = tmp[l, e, here]
        total = (
            wes[l, e, flat] * (near[e, flat, 0:N] - f) * (near2[e, flat, 0:N] - a)
            + wws[l, e, flat] * (near[e, flat, N : 2 * N] - f) * (near2[e, flat, N : 2 * N] - a)
            + wys[l, e, here] * (fl[l, e, north] - f) * (tmp[l, e, north] - a)
            + wys[l, e, south] * (fl[l, e, south] - f) * (tmp[l, e, south] - a)
            + wzs[l, e, flat] * (fl[l, e + 1, here] - f) * (tmp[l, e + 1, here] - a)
            + wzs[l, e - 1, flat] * (fl[l, e - 1, here] - f) * (tmp[l, e - 1, here] - a)
        )
        ab[l, e, flat] = 12.0 * h * h * total

    return inside, clear, optics, per_plane, face, first, second, third, couple


def inner_kernel(where, spectra, absorb_t, half_t, labels, illum, start, meas, *rest):
    state, (own, lit, step, near, near2, sem) = rest[:11], rest[11:]
    fl, hd, wys, tmp, adj, ab, wes, wws, wzs, inv, ms = state
    _, clear, optics, per_plane, face, first, second, third, _ = stages(
        where, spectra, absorb_t, half_t, lit, step, near, near2, state
    )
    copies = [
        pltpu.make_async_copy(labels, own, sem.at[0]),
        pltpu.make_async_copy(start, fl.at[:, pl.ds(HF, NP), pl.ds(PAD, N)], sem.at[1]),
        pltpu.make_async_copy(meas, ms.at[:, pl.ds(HM, NP)], sem.at[2]),
    ]
    for copy in copies:
        copy.start()
    lit[...] = illum[...].astype(F32)
    step[...] = shifts()
    lax.fori_loop(0, EXT, clear, 0)

    def optics_own(p, _):
        for c in range(N // CHUNK):
            optics(own[p, pl.ds(c * CHUNK, CHUNK)], p + HF, c * CHUNK)
        return 0

    copies[0].wait()
    lax.fori_loop(0, NP, optics_own, 0)
    face(HF)
    copies[1].wait()
    per_plane(((HF + 1, HF + NP - 1),), (fl, hd), first)
    copies[2].wait()
    per_plane(((HF + 2, HF + NP - 2),), (tmp,), second)
    per_plane(((HF + 3, HF + NP - 3),), (adj,), third)


def solve_kernel(
    where, spectra, absorb_t, half_t, illum, side_a, bulk_b, straight_b, turned_b, *rest,
):
    fluence, coef_a, coef_b, edge_a, edge_b, *rest = rest[11:]
    outs, state = rest[:6], rest[6:17]
    shared, lit, step, near, near2, sem = rest[17:]
    fl, hd, wys, tmp, adj, ab, wes, wws, wzs, inv, ms = state
    sends, keeps = outs[0::2], outs[1::2]
    inside, _, optics, per_plane, face, first, second, third, couple = stages(
        where, spectra, absorb_t, half_t, lit, step, near, near2, state
    )
    gz = where[0]
    me = where[1]
    odd = lax.rem(gz, 2)
    whole = pl.ds(PAD, N)

    def incoming(bulk, extra, high, number):
        def piece(at, count):
            return bulk.at[pl.ds(at, count)] if at < BULK else extra.at[pl.ds(at - BULK, count)]

        first = 3 + 9 * number
        lights = [
            pltpu.make_async_copy(
                piece(l * HF, HF), fl.at[l, pl.ds(high * (HF + NP), HF), whole], sem.at[first + l]
            )
            for l in range(4)
        ]
        pressures = [
            pltpu.make_async_copy(
                piece(4 * HF + l * HM, HM), ms.at[l, pl.ds(high * (HM + NP), HM)], sem.at[first + 4 + l]
            )
            for l in range(4)
        ]
        classes = pltpu.make_async_copy(
            piece(TOTAL - HF, HF), shared.at[pl.ds(high * HF, HF)], sem.at[first + 8]
        )
        return lights, pressures, classes

    rest_a = side_a.at[pl.ds(BULK, TOTAL - BULK)]
    lights_a, pressures_a, classes_a = incoming(side_a, rest_a, 1 - odd, 0)
    lights_b, pressures_b, classes_b = incoming(bulk_b, straight_b, odd, 1)
    _, turned_pressures, turned_classes = incoming(bulk_b, turned_b, odd, 1)
    label_copies = [classes_a, classes_b]
    meas_copies = pressures_a + pressures_b
    fluence_copies = lights_a + lights_b
    turned = (lax.rem(gz, 8) == 0) | (lax.rem(gz, 8) == 7)
    classes_a.start()

    @pl.when(turned)
    def _():
        turned_classes.start()
        for copy in turned_pressures[2:]:
            copy.start()

    @pl.when(jnp.logical_not(turned))
    def _():
        classes_b.start()
        for copy in pressures_b[2:]:
            copy.start()

    for copy in fluence_copies + pressures_a + pressures_b[:2]:
        copy.start()

    lit[...] = illum[...].astype(F32)
    step[...] = shifts()

    def optics_shared(p, _):
        e = p + jnp.where(p < HF, 0, NP)
        for c in range(N // CHUNK):
            classes = shared[p, pl.ds(c * CHUNK, CHUNK)].astype(jnp.int32)
            optics(classes, e, c * CHUNK)
        return 0

    for copy in label_copies:
        copy.wait()
    lax.fori_loop(0, 2 * HF, optics_shared, 0)
    for copy in fluence_copies:
        copy.wait()

    @pl.when(gz == 0)
    def _():
        fl[:, HF - 1] = jnp.zeros((4, N + 2 * PAD, N), F32)

    @pl.when(gz == 31)
    def _():
        fl[:, HF + NP] = jnp.zeros((4, N + 2 * PAD, N), F32)

    face(0)
    last = HF + NP
    per_plane(((1, HF + 1), (last - 1, EXT - 1)), (fl, hd), first)
    for copy in meas_copies:
        copy.wait()
    per_plane(((2, HF + 2), (last - 2, EXT - 2)), (tmp,), second)
    write = pltpu.make_async_copy(fl.at[:, pl.ds(HF, NP), whole], fluence, sem.at[0])
    write.start()
    for l in range(4):
        tmp[l, HF - 1] = jnp.zeros((N + 2 * PAD, N), F32)
        tmp[l, last] = jnp.zeros((N + 2 * PAD, N), F32)
    per_plane(((HF, HF + 3), (last - 3, last)), (adj,), third)
    per_plane(((HF, last),), (fl, tmp), couple)

    for coef, edge, high in ((coef_a, edge_a, 1 - odd), (coef_b, edge_b, odd)):
        e = HF + high * (NP - 1)
        beyond = e + 2 * high - 1
        face = e + high - 1
        for l in range(4):
            for c in range(N // CHUNK):
                here = pl.ds(PAD + c * CHUNK, CHUNK)
                to = pl.ds(c * CHUNK, CHUNK)
                h = hd[l, e, here]
                edge[l, to] = tmp[l, e, here]
                coef[l, to] = (
                    spectra[l, 4] * 12.0 * h * h * wzs[l, face, to] * (fl[l, beyond, here] - fl[l, e, here])
                )

    for code in range(8):
        rows = pl.ds(pl.multiple_of(PAD + (me ^ code) * ROWS, 8), ROWS)
        flat = pl.ds(pl.multiple_of((me ^ code) * ROWS, 8), ROWS)
        for plane in range(NP):
            e = plane + HF
            common = [fl[l, e, rows] * (ms[l, e - (HF - HM), flat] - tmp[l, e, rows]) for l in range(4)]
            paired = [ab[l, e, flat] for l in range(4)]
            for field in range(5):
                terms = common if field < 4 else paired
                value = spectra[0, field] * terms[0]
                for l in range(1, 4):
                    value = value + spectra[l, field] * terms[l]
                part, index = part_of(plane, field)
                slot = slot_of(part, code)
                if slot >= 4:
                    sends[part][slot - 4, index] = value
                else:
                    keeps[part][slot, index] = value
    write.wait()


def edge_kernel(where, coef_a, coef_b, edge_a, edge_b, send, keep):
    gz, me = where[0], where[1]
    there = jnp.where((gz > 0) & (gz < 31), 1.0, 0.0).astype(F32)
    for code in range(8):
        rows = pl.ds(pl.multiple_of((me ^ code) * ROWS, ROWS), ROWS)
        slot = slot_of(0, code)
        for side, (coef, edge) in enumerate(((coef_a, edge_a), (coef_b, edge_b))):
            value = coef[0, rows] * edge[0, rows]
            for l in range(1, 4):
                value = value + coef[l, rows] * edge[l, rows]
            if side:
                value = value * there
            if slot >= 4:
                send[slot - 4, side] = value
            else:
                keep[slot, side] = value


def squares_kernel(where, late_keep, late_recv, *refs):
    keeps, recvs, owns, sums = refs[:3], refs[3:6], refs[6:9], refs[9]
    odd = lax.rem(where[0], 2)
    total = [jnp.zeros((8, N), F32) for _ in range(5)]
    for plane in range(NP):
        for field in range(5):
            part, index = part_of(plane, field)
            value = keeps[part][0, index] + recvs[part][0, index]
            if field == 4 and plane in (0, NP - 1):
                side = 1 - odd if plane == 0 else odd
                value = value + (late_keep[0, side] + late_recv[0, side])
            owns[part][0, index] = value
            squared = value * value
            total[field] = total[field] + squared[:8] + squared[8:]
    lane = lax.broadcasted_iota(jnp.int32, (1, N), 1)
    row = jnp.zeros((1, N), F32)
    for field in range(5):
        whole = jnp.sum(jnp.sum(total[field], axis=0, keepdims=True), axis=1, keepdims=True)
        row = jnp.where(lane == field, whole, row)
    for target in range(32):
        sums[target] = row


def final_kernel(where, table, labels, *refs):
    pieces, (conc, scat, done, sem) = refs[:12], refs[12:]
    me = where[1]
    cells = 32 * NP * N * N
    extra = PARTS[0][1]
    total = pieces[0][0, extra] + pieces[1][0, extra]
    for i in range(2):
        total = total + pieces[2][i, extra]
    for i in range(4):
        total = total + pieces[3][i, extra]
    factor = -STEP / jnp.sqrt(total / cells + 1e-06)
    factors = [jnp.broadcast_to(factor[:, c : c + 1], (ROWS, N)) for c in range(5)]
    copies = []
    for plane in range(NP):
        for code in range(8):
            rows = pl.ds(pl.multiple_of((me ^ code) * ROWS, ROWS), ROWS)
            classes = labels[plane, rows]
            for field in range(5):
                part, index = part_of(plane, field)
                slot = slot_of(part, code)
                own, one, two, four = pieces[4 * part : 4 * part + 4]
                if slot == 0:
                    grad = own[0, index]
                elif slot == 1:
                    grad = one[0, index]
                elif slot < 4:
                    grad = two[slot - 2, index]
                else:
                    grad = four[slot - 4, index]
                coeff = pick(classes, [table[i, field] for i in range(8)])
                done[field, plane, rows] = coeff * jnp.exp(grad * factors[field])
        copies.append(pltpu.make_async_copy(done.at[0:4, plane], conc.at[:, plane], sem.at[plane, 0]))
        copies.append(pltpu.make_async_copy(done.at[4, plane], scat.at[plane], sem.at[plane, 1]))
        copies[-2].start()
        copies[-1].start()
    for copy in copies:
        copy.wait()


VMEM = pl.BlockSpec(memory_space=pltpu.VMEM)
SMEM = pl.BlockSpec(memory_space=pltpu.SMEM)
ANY = pl.BlockSpec(memory_space=pl.ANY)


def swap(x, code):
    return lax.ppermute(x, "wl", [(i, i ^ code) for i in range(8)])


ON_CHIP = [(i, i ^ 1) for i in range(32)]
OFF_CHIP = [(i, (i + 1 if i % 2 else i - 1) % 32) for i in range(32)]
AROUND = [(i, i - 7 if i % 8 == 7 else i + 7 if i % 8 == 0 else j) for i, j in OFF_CHIP]
ALONG = [(i, i + 8) for i in (0, 8, 16)] + [(i, i - 8) for i in (15, 23, 31)]


def beside(a, b):
    return lax.ppermute(a, "gz", ON_CHIP), lax.ppermute(b, "gz", OFF_CHIP)


def shards(labels, label_table, spectra, illumination, fluence_start, measured):
    where = jnp.stack([lax.axis_index("gz"), lax.axis_index("wl")]).astype(jnp.int32)
    small = pltpu.CompilerParams(vmem_limit_bytes=12 * 2**20)

    def in_hbm(x):
        return pltpu.with_memory_space_constraint(x, pltpu.HBM)

    def in_vmem(x):
        return pltpu.with_memory_space_constraint(x, pltpu.VMEM)

    bulk_b, extra_b, side_a = pl.pallas_call(
        pack_kernel,
        out_shape=[pltpu.VMEM((count, N, N), F32) for count in (BULK, TOTAL - BULK, TOTAL)],
        in_specs=[SMEM] + [ANY] * 3,
        out_specs=[VMEM] * 3,
        scratch_shapes=[pltpu.VMEM((2, HF, N, N), jnp.int32), pltpu.SemaphoreType.DMA((2, 9))],
        compiler_params=small,
        name="pack",
    )(where, *map(in_hbm, (labels, fluence_start, measured)))
    bulk_b = lax.ppermute(bulk_b, "gz", OFF_CHIP)
    straight_b = lax.ppermute(extra_b, "gz", AROUND)
    side_a = lax.ppermute(side_a, "gz", ON_CHIP)
    turned_b = lax.ppermute(straight_b, "gz", ALONG)
    side_a, bulk_b, straight_b, turned_b = map(in_vmem, (side_a, bulk_b, straight_b, turned_b))

    absorb_t = spectra[:, 0, None] * label_table[None, :, 0]
    for c in range(1, 4):
        absorb_t = absorb_t + spectra[:, c, None] * label_table[None, :, c]
    half_t = 0.5 / (3.0 * (absorb_t + spectra[:, 4, None] * label_table[None, :, 4]))

    sizes = [last - first for first, last in PARTS]
    held = (
        [pltpu.VMEM((4, EXT, N + 2 * PAD, N), F32)] * 5
        + [pltpu.VMEM((4, EXT, N, N), F32)] * 5
        + [pltpu.VMEM((4, NP + 2 * HM, N, N), F32)]
    )
    work = [
        pltpu.VMEM((N, N), F32),
        pltpu.VMEM((2 * N, 2 * N), jnp.bfloat16),
        pltpu.VMEM((EXT, N, 2 * N), F32),
        pltpu.VMEM((EXT, N, 2 * N), F32),
    ]
    state = pl.pallas_call(
        inner_kernel,
        out_shape=held,
        in_specs=[SMEM] * 4 + [ANY] + [VMEM] + [ANY] * 2,
        out_specs=[VMEM] * 11,
        scratch_shapes=[pltpu.VMEM((NP, N, N), jnp.int32)] + work + [pltpu.SemaphoreType.DMA((3,))],
        compiler_params=small,
        name="inner",
    )(where, spectra, absorb_t, half_t, in_hbm(labels), illumination, *map(in_hbm, (fluence_start, measured)))
    fluence, coef_a, coef_b, edge_a, edge_b, *out = pl.pallas_call(
        solve_kernel,
        out_shape=[jax.ShapeDtypeStruct((4, NP, N, N), F32)]
        + [pltpu.VMEM((4, N, N), F32)] * 4
        + [pltpu.VMEM((4, size, ROWS, N), F32) for size in sizes for _ in range(2)]
        + held,
        in_specs=[SMEM] * 4 + [VMEM] + [ANY] * 4 + [VMEM] * 11,
        out_specs=[ANY] + [VMEM] * 21,
        input_output_aliases={9 + i: 11 + i for i in range(11)},
        scratch_shapes=[pltpu.VMEM((2 * HF, N, N), F32)] + work + [pltpu.SemaphoreType.DMA((21,))],
        compiler_params=small,
        name="solve",
    )(where, spectra, absorb_t, half_t, illumination, side_a, bulk_b, straight_b, turned_b, *map(in_vmem, state))
    out = out[:6]
    sends = list(out[0::2])
    keeps = list(out[1::2])

    far_a, far_b = beside(edge_a, edge_b)
    for phase in range(2):
        recvs = [swap(sends[q], GENS[ORDERS[q][phase]]) for q in range(3)]
        half = keeps[0].shape[0] // 2
        sends = [keeps[q][half:] + recvs[q][half:] for q in range(3)]
        keeps = [keeps[q][:half] + recvs[q][:half] for q in range(3)]
        if phase == 0:
            far_a, far_b = lax.optimization_barrier((far_a, far_b, *sends))[:2]
    recvs = [swap(sends[q], GENS[ORDERS[q][2]]) for q in range(3)]

    late_send, late_keep = pl.pallas_call(
        edge_kernel,
        out_shape=[jax.ShapeDtypeStruct((4, 2, ROWS, N), F32)] * 2,
        in_specs=[SMEM] + [VMEM] * 4,
        out_specs=[VMEM] * 2,
        compiler_params=small,
        name="edge",
    )(where, coef_a, coef_b, far_a, far_b)
    for phase in range(2):
        late_recv = swap(late_send, GENS[ORDERS[0][phase]])
        half = late_keep.shape[0] // 2
        late_send = late_keep[half:] + late_recv[half:]
        late_keep = late_keep[:half] + late_recv[:half]
    late_recv = swap(late_send, GENS[ORDERS[0][2]])

    *owns, sums = pl.pallas_call(
        squares_kernel,
        out_shape=[jax.ShapeDtypeStruct((1, size, ROWS, N), F32) for size in sizes]
        + [jax.ShapeDtypeStruct((32, 1, N), F32)],
        in_specs=[SMEM] + [VMEM] * 8,
        out_specs=[VMEM] * 4,
        compiler_params=small,
        name="squares",
    )(where, late_keep, late_recv, *keeps, *recvs)

    steps = {q: [owns[q]] for q in (1, 2)}
    for phase in (2, 1, 0):
        for q in (1, 2):
            have = steps[q]
            mine = have[0] if len(have) == 1 else jnp.concatenate(have)
            have.append(swap(mine, GENS[ORDERS[q][phase]]))
    slab = jnp.sum(lax.all_to_all(sums, "gz", 0, 0), axis=0)
    steps[0] = [jnp.concatenate([owns[0], jnp.broadcast_to(slab[None, None], (1, 1, ROWS, N))], axis=1)]
    for phase in (2, 1, 0):
        have = steps[0]
        mine = have[0] if len(have) == 1 else jnp.concatenate(have)
        have.append(swap(mine, GENS[ORDERS[0][phase]]))
    pieces = steps[0] + steps[1] + steps[2]
    conc, scat = pl.pallas_call(
        final_kernel,
        out_shape=[jax.ShapeDtypeStruct((4, NP, N, N), F32), jax.ShapeDtypeStruct((NP, N, N), F32)],
        in_specs=[SMEM] * 2 + [VMEM] * 13,
        out_specs=[ANY] * 2,
        scratch_shapes=[pltpu.VMEM((5, NP, N, N), F32), pltpu.SemaphoreType.DMA((NP, 2))],
        compiler_params=pltpu.CompilerParams(vmem_limit_bytes=32 * 2**20),
        name="final",
    )(where, label_table, labels, *pieces)
    return fluence, conc, scat


def solution(mesh):
    in_specs = (
        P("gz", None, None),
        P(),
        P("wl", None),
        P(),
        P("wl", "gz", None, None),
        P("wl", "gz", None, None),
    )
    out_specs = (P("wl", "gz", None, None), P(None, "gz", None, None), P("gz", None, None))
    return jax.shard_map(shards, mesh=mesh, in_specs=in_specs, out_specs=out_specs, check_vma=False)
```

```python
import functools

import jax
import jax.numpy as jnp
from jax import lax
from jax.experimental import pallas as pl
from jax.experimental.pallas import tpu as pltpu
from jax.sharding import PartitionSpec as P

STEP = 0.3
HF = 3
HM = 1
NP = 8
EXT = NP + 2 * HF
TOTAL = 4 * (HF + HM) + HF
BULK = 4 * HF + 2 * HM
N = 128
PAD = 8
CHUNK = 32
F32 = jnp.float32

GENS = (2, 6, 1)
ORDERS = ((0, 1, 2), (1, 2, 0), (2, 0, 1))
PARTS = ((0, 14), (14, 27), (27, 40))
ROWS = 16


def code_of(part, slot):
    order = ORDERS[part]
    bits = (slot >> 2 & 1, slot >> 1 & 1, slot & 1)
    code = 0
    for dim, bit in zip(order, bits):
        code ^= GENS[dim] * bit
    return code


def slot_of(part, code):
    return [code_of(part, slot) for slot in range(8)].index(code)


def part_of(plane, field):
    at = plane * 5 + field
    for part, (first, last) in enumerate(PARTS):
        if at < last:
            return part, at - first


def shifts():
    source = lax.broadcasted_iota(jnp.int32, (2 * N, 2 * N), 0)
    target = lax.broadcasted_iota(jnp.int32, (2 * N, 2 * N), 1)
    x = jnp.where(source >= N, source - N, source)
    ahead = (target < N) & (x == target + 1)
    behind = (target >= N) & (x == target - N - 1)
    return jnp.where(ahead | behind, 1.0, 0.0).astype(jnp.bfloat16)


def two_terms(v):
    high = v.astype(jnp.bfloat16)
    low = (v - high.astype(F32)).astype(jnp.bfloat16)
    return jnp.concatenate([high, low], axis=1)


def pick(classes, entries):
    bit0 = (classes & 1) != 0
    bit1 = (classes & 2) != 0
    bit2 = (classes & 4) != 0
    low = [jnp.where(bit0, entries[2 * i + 1], entries[2 * i]) for i in range(4)]
    mid = [jnp.where(bit1, low[2 * i + 1], low[2 * i]) for i in range(2)]
    return jnp.where(bit2, mid[1], mid[0])


def pack_kernel(where, labels, start, meas, bulk_b, extra_b, side_a, ints, sem):
    odd = lax.rem(where[0], 2)
    copies = []
    for side, flip in enumerate((odd, 1 - odd)):

        def place(at, count):
            if side == 1:
                return side_a.at[pl.ds(at, count)]
            return bulk_b.at[pl.ds(at, count)] if at < BULK else extra_b.at[pl.ds(at - BULK, count)]

        copies.append(
            pltpu.make_async_copy(labels.at[pl.ds(flip * (NP - HF), HF)], ints.at[side], sem.at[side, 8])
        )
        for l in range(4):
            copies.append(
                pltpu.make_async_copy(
                    start.at[l, pl.ds(flip * (NP - HF), HF)], place(l * HF, HF), sem.at[side, l]
                )
            )
            copies.append(
                pltpu.make_async_copy(
                    meas.at[l, pl.ds(flip * (NP - HM), HM)], place(4 * HF + l * HM, HM), sem.at[side, 4 + l]
                )
            )
    for copy in copies:
        copy.start()
    for copy in copies:
        copy.wait()
    extra_b[TOTAL - HF - BULK : TOTAL - BULK] = ints[0].astype(F32)
    side_a[TOTAL - HF : TOTAL] = ints[1].astype(F32)


def stages(where, spectra, absorb_t, half_t, lit, step, near, near2, state):
    fl, hd, wys, tmp, adj, ab, wes, wws, wzs, inv, ms = state
    gz = where[0]
    pad = jnp.zeros((PAD, N), F32)

    def inside(e):
        z = gz * NP + e - HF
        return jnp.where((z >= 0) & (z < 32 * NP), 1.0, 0.0).astype(F32)

    def clear(e, _):
        for l in range(4):
            for field in (fl, tmp, adj, hd):
                field[l, e, 0:PAD] = pad
                field[l, e, PAD + N : 2 * PAD + N] = pad
        return 0

    def optics(classes, e, r):
        there = inside(e)
        flat = pl.ds(r, CHUNK)
        rows = pl.ds(PAD + r, CHUNK)
        for l in range(4):
            ab[l, e, flat] = pick(classes, [absorb_t[l, i] for i in range(8)])
            hd[l, e, rows] = pick(classes, [half_t[l, i] * there for i in range(8)])

    def per_plane(ranges, fields, body):
        def spread(to, field, l):
            parts = [field[l, a:b, PAD : PAD + N].reshape((b - a) * N, N) for a, b in ranges]
            rows = parts[0] if len(parts) == 1 else jnp.concatenate(parts)
            both = jnp.dot(two_terms(rows), step[...], preferred_element_type=F32)
            at = 0
            for a, b in ranges:
                to[a:b] = both[at : at + (b - a) * N].reshape(b - a, N, 2 * N)
                at += (b - a) * N

        def outerloop(l, _):
            for to, field in zip((near, near2), fields):
                spread(to, field, l)

            def innerloop(e, _):
                for c in range(N // CHUNK):
                    body(l, e, c * CHUNK)
                return 0

            for a, b in ranges:
                lax.fori_loop(a, b, innerloop, 0)
            return 0

        lax.fori_loop(0, 4, outerloop, 0)

    def face(e):
        for l in range(4):
            for c in range(N // CHUNK):
                here = pl.ds(PAD + c * CHUNK, CHUNK)
                wzs[l, e, pl.ds(c * CHUNK, CHUNK)] = hd[l, e, here] + hd[l, e + 1, here]

    def moved(field, l, e, r):
        flat = pl.ds(r, CHUNK)
        here = pl.ds(PAD + r, CHUNK)
        north = pl.ds(PAD + r + 1, CHUNK)
        south = pl.ds(PAD + r - 1, CHUNK)
        return (
            wzs[l, e, flat] * field[l, e + 1, here]
            + wzs[l, e - 1, flat] * field[l, e - 1, here]
            + wys[l, e, here] * field[l, e, north]
            + wys[l, e, south] * field[l, e, south]
            + wes[l, e, flat] * near[e, flat, 0:N]
            + wws[l, e, flat] * near[e, flat, N : 2 * N]
        )

    def first(l, e, r):
        flat = pl.ds(r, CHUNK)
        here = pl.ds(PAD + r, CHUNK)
        north_rows = pl.ds(PAD + r + 1, CHUNK)
        south_rows = pl.ds(PAD + r - 1, CHUNK)
        h = hd[l, e, here]
        north = h + hd[l, e, north_rows]
        south = h + hd[l, e, south_rows]
        above = h + hd[l, e + 1, here]
        below = wzs[l, e - 1, flat]
        east = h + near2[e, flat, 0:N]
        west = h + near2[e, flat, N : 2 * N]
        if r == 0:
            wys[l, e, 0:PAD] = jnp.broadcast_to(h[0:1], (PAD, N))
        wys[l, e, here] = north
        wzs[l, e, flat] = above
        wes[l, e, flat] = east
        wws[l, e, flat] = west
        total = ab[l, e, flat] + above + below + north + south + east + west
        scale = inside(e) / total
        inv[l, e, flat] = scale
        flow = (
            above * fl[l, e + 1, here]
            + below * fl[l, e - 1, here]
            + north * fl[l, e, north_rows]
            + south * fl[l, e, south_rows]
            + east * near[e, flat, 0:N]
            + west * near[e, flat, N : 2 * N]
        )
        tmp[l, e, here] = (spectra[l, 5] * lit[flat] + flow) * scale

    def second(l, e, r):
        flat = pl.ds(r, CHUNK)
        here = pl.ds(PAD + r, CHUNK)
        scale = inv[l, e, flat]
        f = (spectra[l, 5] * lit[flat] + moved(tmp, l, e, r)) * scale
        fl[l, e, here] = f
        absorb = ab[l, e, flat]
        misfit = absorb * f - ms[l, e - (HF - HM), flat]
        ms[l, e - (HF - HM), flat] = misfit
        adj[l, e, here] = absorb * misfit * scale

    def third(l, e, r):
        flat = pl.ds(r, CHUNK)
        here = pl.ds(PAD + r, CHUNK)
        tmp[l, e, here] = (ab[l, e, flat] * ms[l, e - (HF - HM), flat] + moved(adj, l, e, r)) * inv[l, e, flat]

    def couple(l, e, r):
        flat = pl.ds(r, CHUNK)
        here = pl.ds(PAD + r, CHUNK)
        north = pl.ds(PAD + r + 1, CHUNK)
        south = pl.ds(PAD + r - 1, CHUNK)
        h = hd[l, e, here]
        f = fl[l, e, here]
        a = tmp[l, e, here]
        total = (
            wes[l, e, flat] * (near[e, flat, 0:N] - f) * (near2[e, flat, 0:N] - a)
            + wws[l, e, flat] * (near[e, flat, N : 2 * N] - f) * (near2[e, flat, N : 2 * N] - a)
            + wys[l, e, here] * (fl[l, e, north] - f) * (tmp[l, e, north] - a)
            + wys[l, e, south] * (fl[l, e, south] - f) * (tmp[l, e, south] - a)
            + wzs[l, e, flat] * (fl[l, e + 1, here] - f) * (tmp[l, e + 1, here] - a)
            + wzs[l, e - 1, flat] * (fl[l, e - 1, here] - f) * (tmp[l, e - 1, here] - a)
        )
        ab[l, e, flat] = 12.0 * h * h * total

    return inside, clear, optics, per_plane, face, first, second, third, couple


def inner_kernel(where, spectra, absorb_t, half_t, labels, illum, start, meas, *rest):
    state, (own, lit, step, near, near2, sem) = rest[:11], rest[11:]
    fl, hd, wys, tmp, adj, ab, wes, wws, wzs, inv, ms = state
    _, clear, optics, per_plane, face, first, second, third, _ = stages(
        where, spectra, absorb_t, half_t, lit, step, near, near2, state
    )
    copies = [
        pltpu.make_async_copy(labels, own, sem.at[0]),
        pltpu.make_async_copy(start, fl.at[:, pl.ds(HF, NP), pl.ds(PAD, N)], sem.at[1]),
        pltpu.make_async_copy(meas, ms.at[:, pl.ds(HM, NP)], sem.at[2]),
    ]
    for copy in copies:
        copy.start()
    lit[...] = illum[...].astype(F32)
    step[...] = shifts()
    lax.fori_loop(0, EXT, clear, 0)

    def optics_own(p, _):
        for c in range(N // CHUNK):
            optics(own[p, pl.ds(c * CHUNK, CHUNK)], p + HF, c * CHUNK)
        return 0

    copies[0].wait()
    lax.fori_loop(0, NP, optics_own, 0)
    face(HF)
    copies[1].wait()
    per_plane(((HF + 1, HF + NP - 1),), (fl, hd), first)
    copies[2].wait()
    per_plane(((HF + 2, HF + NP - 2),), (tmp,), second)
    per_plane(((HF + 3, HF + NP - 3),), (adj,), third)


def solve_kernel(
    where, spectra, absorb_t, half_t, illum, side_a, bulk_b, straight_b, turned_b, *rest,
):
    fluence, coef_a, coef_b, edge_a, edge_b, *rest = rest[11:]
    outs, state = rest[:6], rest[6:17]
    shared, lit, step, near, near2, sem = rest[17:]
    fl, hd, wys, tmp, adj, ab, wes, wws, wzs, inv, ms = state
    sends, keeps = outs[0::2], outs[1::2]
    inside, _, optics, per_plane, face, first, second, third, couple = stages(
        where, spectra, absorb_t, half_t, lit, step, near, near2, state
    )
    gz = where[0]
    me = where[1]
    odd = lax.rem(gz, 2)
    whole = pl.ds(PAD, N)

    def incoming(bulk, extra, high, number):
        def piece(at, count):
            return bulk.at[pl.ds(at, count)] if at < BULK else extra.at[pl.ds(at - BULK, count)]

        first = 3 + 9 * number
        lights = [
            pltpu.make_async_copy(
                piece(l * HF, HF), fl.at[l, pl.ds(high * (HF + NP), HF), whole], sem.at[first + l]
            )
            for l in range(4)
        ]
        pressures = [
            pltpu.make_async_copy(
                piece(4 * HF + l * HM, HM), ms.at[l, pl.ds(high * (HM + NP), HM)], sem.at[first + 4 + l]
            )
            for l in range(4)
        ]
        classes = pltpu.make_async_copy(
            piece(TOTAL - HF, HF), shared.at[pl.ds(high * HF, HF)], sem.at[first + 8]
        )
        return lights, pressures, classes

    rest_a = side_a.at[pl.ds(BULK, TOTAL - BULK)]
    lights_a, pressures_a, classes_a = incoming(side_a, rest_a, 1 - odd, 0)
    lights_b, pressures_b, classes_b = incoming(bulk_b, straight_b, odd, 1)
    _, turned_pressures, turned_classes = incoming(bulk_b, turned_b, odd, 1)
    label_copies = [classes_a, classes_b]
    meas_copies = pressures_a + pressures_b
    fluence_copies = lights_a + lights_b
    turned = (lax.rem(gz, 8) == 0) | (lax.rem(gz, 8) == 7)
    classes_a.start()

    @pl.when(turned)
    def _():
        turned_classes.start()
        for copy in turned_pressures[2:]:
            copy.start()

    @pl.when(jnp.logical_not(turned))
    def _():
        classes_b.start()
        for copy in pressures_b[2:]:
            copy.start()

    for copy in fluence_copies + pressures_a + pressures_b[:2]:
        copy.start()

    lit[...] = illum[...].astype(F32)
    step[...] = shifts()

    def optics_shared(p, _):
        e = p + jnp.where(p < HF, 0, NP)
        for c in range(N // CHUNK):
            classes = shared[p, pl.ds(c * CHUNK, CHUNK)].astype(jnp.int32)
            optics(classes, e, c * CHUNK)
        return 0

    for copy in label_copies:
        copy.wait()
    lax.fori_loop(0, 2 * HF, optics_shared, 0)
    for copy in fluence_copies:
        copy.wait()

    @pl.when(gz == 0)
    def _():
        fl[:, HF - 1] = jnp.zeros((4, N + 2 * PAD, N), F32)

    @pl.when(gz == 31)
    def _():
        fl[:, HF + NP] = jnp.zeros((4, N + 2 * PAD, N), F32)

    face(0)
    last = HF + NP
    per_plane(((1, HF + 1), (last - 1, EXT - 1)), (fl, hd), first)
    for copy in meas_copies:
        copy.wait()
    per_plane(((2, HF + 2), (last - 2, EXT - 2)), (tmp,), second)
    write = pltpu.make_async_copy(fl.at[:, pl.ds(HF, NP), whole], fluence, sem.at[0])
    write.start()
    for l in range(4):
        tmp[l, HF - 1] = jnp.zeros((N + 2 * PAD, N), F32)
        tmp[l, last] = jnp.zeros((N + 2 * PAD, N), F32)
    per_plane(((HF, HF + 3), (last - 3, last)), (adj,), third)
    per_plane(((HF, last),), (fl, tmp), couple)

    for coef, edge, high in ((coef_a, edge_a, 1 - odd), (coef_b, edge_b, odd)):
        e = HF + high * (NP - 1)
        beyond = e + 2 * high - 1
        face = e + high - 1
        for l in range(4):
            for c in range(N // CHUNK):
                here = pl.ds(PAD + c * CHUNK, CHUNK)
                to = pl.ds(c * CHUNK, CHUNK)
                h = hd[l, e, here]
                edge[l, to] = tmp[l, e, here]
                coef[l, to] = (
                    spectra[l, 4] * 12.0 * h * h * wzs[l, face, to] * (fl[l, beyond, here] - fl[l, e, here])
                )

    for code in range(8):
        rows = pl.ds(pl.multiple_of(PAD + (me ^ code) * ROWS, 8), ROWS)
        flat = pl.ds(pl.multiple_of((me ^ code) * ROWS, 8), ROWS)
        for plane in range(NP):
            e = plane + HF
            common = [fl[l, e, rows] * (ms[l, e - (HF - HM), flat] - tmp[l, e, rows]) for l in range(4)]
            paired = [ab[l, e, flat] for l in range(4)]
            for field in range(5):
                terms = common if field < 4 else paired
                value = spectra[0, field] * terms[0]
                for l in range(1, 4):
                    value = value + spectra[l, field] * terms[l]
                part, index = part_of(plane, field)
                slot = slot_of(part, code)
                if slot >= 4:
                    sends[part][slot - 4, index] = value
                else:
                    keeps[part][slot, index] = value
    write.wait()


def edge_kernel(where, coef_a, coef_b, edge_a, edge_b, send, keep):
    gz, me = where[0], where[1]
    there = jnp.where((gz > 0) & (gz < 31), 1.0, 0.0).astype(F32)
    for code in range(8):
        rows = pl.ds(pl.multiple_of((me ^ code) * ROWS, ROWS), ROWS)
        slot = slot_of(0, code)
        for side, (coef, edge) in enumerate(((coef_a, edge_a), (coef_b, edge_b))):
            value = coef[0, rows] * edge[0, rows]
            for l in range(1, 4):
                value = value + coef[l, rows] * edge[l, rows]
            if side:
                value = value * there
            if slot >= 4:
                send[slot - 4, side] = value
            else:
                keep[slot, side] = value


def squares_kernel(where, late_keep, late_recv, *refs):
    keeps, recvs, owns, sums = refs[:3], refs[3:6], refs[6:9], refs[9]
    odd = lax.rem(where[0], 2)
    total = [jnp.zeros((8, N), F32) for _ in range(5)]
    for plane in range(NP):
        for field in range(5):
            part, index = part_of(plane, field)
            value = keeps[part][0, index] + recvs[part][0, index]
            if field == 4 and plane in (0, NP - 1):
                side = 1 - odd if plane == 0 else odd
                value = value + (late_keep[0, side] + late_recv[0, side])
            owns[part][0, index] = value
            squared = value * value
            total[field] = total[field] + squared[:8] + squared[8:]
    lane = lax.broadcasted_iota(jnp.int32, (1, N), 1)
    row = jnp.zeros((1, N), F32)
    for field in range(5):
        whole = jnp.sum(jnp.sum(total[field], axis=0, keepdims=True), axis=1, keepdims=True)
        row = jnp.where(lane == field, whole, row)
    for target in range(32):
        sums[target] = row


def share_kernel(own, sums, out):
    out[0, 0 : PARTS[0][1]] = own[0]
    slab = sums[0]
    for source in range(1, 32):
        slab = slab + sums[source]
    out[0, PARTS[0][1]] = jnp.broadcast_to(slab, (ROWS, N))


def final_kernel(where, table, labels, *refs):
    pieces, (conc, scat, done, sem) = refs[:12], refs[12:]
    me = where[1]
    cells = 32 * NP * N * N
    extra = PARTS[0][1]
    total = pieces[0][0, extra] + pieces[1][0, extra]
    for i in range(2):
        total = total + pieces[2][i, extra]
    for i in range(4):
        total = total + pieces[3][i, extra]
    factor = -STEP / jnp.sqrt(total / cells + 1e-06)
    factors = [jnp.broadcast_to(factor[:, c : c + 1], (ROWS, N)) for c in range(5)]
    copies = []
    for plane in range(NP):
        for code in range(8):
            rows = pl.ds(pl.multiple_of((me ^ code) * ROWS, ROWS), ROWS)
            classes = labels[plane, rows]
            for field in range(5):
                part, index = part_of(plane, field)
                slot = slot_of(part, code)
                own, one, two, four = pieces[4 * part : 4 * part + 4]
                if slot == 0:
                    grad = own[0, index]
                elif slot == 1:
                    grad = one[0, index]
                elif slot < 4:
                    grad = two[slot - 2, index]
                else:
                    grad = four[slot - 4, index]
                coeff = pick(classes, [table[i, field] for i in range(8)])
                done[field, plane, rows] = coeff * jnp.exp(grad * factors[field])
        copies.append(pltpu.make_async_copy(done.at[0:4, plane], conc.at[:, plane], sem.at[plane, 0]))
        copies.append(pltpu.make_async_copy(done.at[4, plane], scat.at[plane], sem.at[plane, 1]))
        copies[-2].start()
        copies[-1].start()
    for copy in copies:
        copy.wait()


VMEM = pl.BlockSpec(memory_space=pltpu.VMEM)
SMEM = pl.BlockSpec(memory_space=pltpu.SMEM)
ANY = pl.BlockSpec(memory_space=pl.ANY)


def swap(x, code):
    return lax.ppermute(x, "wl", [(i, i ^ code) for i in range(8)])


ON_CHIP = [(i, i ^ 1) for i in range(32)]
OFF_CHIP = [(i, (i + 1 if i % 2 else i - 1) % 32) for i in range(32)]
AROUND = [(i, i - 7 if i % 8 == 7 else i + 7 if i % 8 == 0 else j) for i, j in OFF_CHIP]
ALONG = [(i, i + 8) for i in (0, 8, 16)] + [(i, i - 8) for i in (15, 23, 31)]


def beside(a, b):
    return lax.ppermute(a, "gz", ON_CHIP), lax.ppermute(b, "gz", OFF_CHIP)


def shards(labels, label_table, spectra, illumination, fluence_start, measured):
    where = jnp.stack([lax.axis_index("gz"), lax.axis_index("wl")]).astype(jnp.int32)
    small = pltpu.CompilerParams(vmem_limit_bytes=12 * 2**20)

    def in_hbm(x):
        return pltpu.with_memory_space_constraint(x, pltpu.HBM)

    def in_vmem(x):
        return pltpu.with_memory_space_constraint(x, pltpu.VMEM)

    bulk_b, extra_b, side_a = pl.pallas_call(
        pack_kernel,
        out_shape=[pltpu.VMEM((count, N, N), F32) for count in (BULK, TOTAL - BULK, TOTAL)],
        in_specs=[SMEM] + [ANY] * 3,
        out_specs=[VMEM] * 3,
        scratch_shapes=[pltpu.VMEM((2, HF, N, N), jnp.int32), pltpu.SemaphoreType.DMA((2, 9))],
        compiler_params=small,
        name="pack",
    )(where, *map(in_hbm, (labels, fluence_start, measured)))
    bulk_b = lax.ppermute(bulk_b, "gz", OFF_CHIP)
    straight_b = lax.ppermute(extra_b, "gz", AROUND)
    side_a = lax.ppermute(side_a, "gz", ON_CHIP)
    turned_b = lax.ppermute(straight_b, "gz", ALONG)
    side_a, bulk_b, straight_b, turned_b = map(in_vmem, (side_a, bulk_b, straight_b, turned_b))

    absorb_t = spectra[:, 0, None] * label_table[None, :, 0]
    for c in range(1, 4):
        absorb_t = absorb_t + spectra[:, c, None] * label_table[None, :, c]
    half_t = 0.5 / (3.0 * (absorb_t + spectra[:, 4, None] * label_table[None, :, 4]))

    sizes = [last - first for first, last in PARTS]
    held = (
        [pltpu.VMEM((4, EXT, N + 2 * PAD, N), F32)] * 5
        + [pltpu.VMEM((4, EXT, N, N), F32)] * 5
        + [pltpu.VMEM((4, NP + 2 * HM, N, N), F32)]
    )
    work = [
        pltpu.VMEM((N, N), F32),
        pltpu.VMEM((2 * N, 2 * N), jnp.bfloat16),
        pltpu.VMEM((EXT, N, 2 * N), F32),
        pltpu.VMEM((EXT, N, 2 * N), F32),
    ]
    state = pl.pallas_call(
        inner_kernel,
        out_shape=held,
        in_specs=[SMEM] * 4 + [ANY] + [VMEM] + [ANY] * 2,
        out_specs=[VMEM] * 11,
        scratch_shapes=[pltpu.VMEM((NP, N, N), jnp.int32)] + work + [pltpu.SemaphoreType.DMA((3,))],
        compiler_params=small,
        name="inner",
    )(where, spectra, absorb_t, half_t, in_hbm(labels), illumination, *map(in_hbm, (fluence_start, measured)))
    fluence, coef_a, coef_b, edge_a, edge_b, *out = pl.pallas_call(
        solve_kernel,
        out_shape=[jax.ShapeDtypeStruct((4, NP, N, N), F32)]
        + [pltpu.VMEM((4, N, N), F32)] * 4
        + [pltpu.VMEM((4, size, ROWS, N), F32) for size in sizes for _ in range(2)]
        + held,
        in_specs=[SMEM] * 4 + [VMEM] + [ANY] * 4 + [VMEM] * 11,
        out_specs=[ANY] + [VMEM] * 21,
        input_output_aliases={9 + i: 11 + i for i in range(11)},
        scratch_shapes=[pltpu.VMEM((2 * HF, N, N), F32)] + work + [pltpu.SemaphoreType.DMA((21,))],
        compiler_params=small,
        name="solve",
    )(where, spectra, absorb_t, half_t, illumination, side_a, bulk_b, straight_b, turned_b, *map(in_vmem, state))
    out = out[:6]
    sends = list(out[0::2])
    keeps = list(out[1::2])

    far_a, far_b = beside(edge_a, edge_b)
    for phase in range(2):
        recvs = [swap(sends[q], GENS[ORDERS[q][phase]]) for q in range(3)]
        half = keeps[0].shape[0] // 2
        sends = [keeps[q][half:] + recvs[q][half:] for q in range(3)]
        keeps = [keeps[q][:half] + recvs[q][:half] for q in range(3)]
        if phase == 0:
            far_a, far_b = lax.optimization_barrier((far_a, far_b, *sends))[:2]
    recvs = [swap(sends[q], GENS[ORDERS[q][2]]) for q in range(3)]

    late_send, late_keep = pl.pallas_call(
        edge_kernel,
        out_shape=[jax.ShapeDtypeStruct((4, 2, ROWS, N), F32)] * 2,
        in_specs=[SMEM] + [VMEM] * 4,
        out_specs=[VMEM] * 2,
        compiler_params=small,
        name="edge",
    )(where, coef_a, coef_b, far_a, far_b)
    for phase in range(2):
        late_recv = swap(late_send, GENS[ORDERS[0][phase]])
        half = late_keep.shape[0] // 2
        late_send = late_keep[half:] + late_recv[half:]
        late_keep = late_keep[:half] + late_recv[:half]
    late_recv = swap(late_send, GENS[ORDERS[0][2]])

    *owns, sums = pl.pallas_call(
        squares_kernel,
        out_shape=[jax.ShapeDtypeStruct((1, size, ROWS, N), F32) for size in sizes]
        + [jax.ShapeDtypeStruct((32, 1, N), F32)],
        in_specs=[SMEM] + [VMEM] * 8,
        out_specs=[VMEM] * 4,
        compiler_params=small,
        name="squares",
    )(where, late_keep, late_recv, *keeps, *recvs)

    steps = {q: [owns[q]] for q in (1, 2)}
    for phase in (2, 1, 0):
        for q in (1, 2):
            have = steps[q]
            mine = have[0] if len(have) == 1 else jnp.concatenate(have)
            have.append(swap(mine, GENS[ORDERS[q][phase]]))
    shared = pl.pallas_call(
        share_kernel,
        out_shape=jax.ShapeDtypeStruct((1, sizes[0] + 1, ROWS, N), F32),
        in_specs=[VMEM] * 2,
        out_specs=VMEM,
        compiler_params=small,
        name="share",
    )(owns[0], lax.all_to_all(sums, "gz", 0, 0))
    steps[0] = [shared]
    for phase in (2, 1, 0):
        have = steps[0]
        mine = have[0] if len(have) == 1 else jnp.concatenate(have)
        have.append(swap(mine, GENS[ORDERS[0][phase]]))
    pieces = steps[0] + steps[1] + steps[2]
    conc, scat = pl.pallas_call(
        final_kernel,
        out_shape=[jax.ShapeDtypeStruct((4, NP, N, N), F32), jax.ShapeDtypeStruct((NP, N, N), F32)],
        in_specs=[SMEM] * 2 + [VMEM] * 13,
        out_specs=[ANY] * 2,
        scratch_shapes=[pltpu.VMEM((5, NP, N, N), F32), pltpu.SemaphoreType.DMA((NP, 2))],
        compiler_params=pltpu.CompilerParams(vmem_limit_bytes=32 * 2**20),
        name="final",
    )(where, label_table, labels, *pieces)
    return fluence, conc, scat


def solution(mesh):
    in_specs = (
        P("gz", None, None),
        P(),
        P("wl", None),
        P(),
        P("wl", "gz", None, None),
        P("wl", "gz", None, None),
    )
    out_specs = (P("wl", "gz", None, None), P(None, "gz", None, None), P("gz", None, None))
    return jax.shard_map(shards, mesh=mesh, in_specs=in_specs, out_specs=out_specs, check_vma=False)
```

```python
import functools

import jax
import jax.numpy as jnp
from jax import lax
from jax.experimental import pallas as pl
from jax.experimental.pallas import tpu as pltpu
from jax.sharding import PartitionSpec as P

STEP = 0.3
HF = 3
HM = 1
NP = 8
EXT = NP + 2 * HF
TOTAL = 4 * (HF + HM) + HF
BULK = 4 * HF + 2 * HM
N = 128
PAD = 8
CHUNK = 64
F32 = jnp.float32

GENS = (2, 6, 1)
ORDERS = ((0, 1, 2), (1, 2, 0), (2, 0, 1))
PARTS = ((0, 14), (14, 27), (27, 40))
ROWS = 16


def code_of(part, slot):
    order = ORDERS[part]
    bits = (slot >> 2 & 1, slot >> 1 & 1, slot & 1)
    code = 0
    for dim, bit in zip(order, bits):
        code ^= GENS[dim] * bit
    return code


def slot_of(part, code):
    return [code_of(part, slot) for slot in range(8)].index(code)


def part_of(plane, field):
    at = plane * 5 + field
    for part, (first, last) in enumerate(PARTS):
        if at < last:
            return part, at - first


def shifts():
    source = lax.broadcasted_iota(jnp.int32, (2 * N, 2 * N), 0)
    target = lax.broadcasted_iota(jnp.int32, (2 * N, 2 * N), 1)
    x = jnp.where(source >= N, source - N, source)
    ahead = (target < N) & (x == target + 1)
    behind = (target >= N) & (x == target - N - 1)
    return jnp.where(ahead | behind, 1.0, 0.0).astype(jnp.bfloat16)


def two_terms(v):
    high = v.astype(jnp.bfloat16)
    low = (v - high.astype(F32)).astype(jnp.bfloat16)
    return jnp.concatenate([high, low], axis=1)


def pick(classes, entries):
    bit0 = (classes & 1) != 0
    bit1 = (classes & 2) != 0
    bit2 = (classes & 4) != 0
    low = [jnp.where(bit0, entries[2 * i + 1], entries[2 * i]) for i in range(4)]
    mid = [jnp.where(bit1, low[2 * i + 1], low[2 * i]) for i in range(2)]
    return jnp.where(bit2, mid[1], mid[0])


def pack_kernel(where, labels, start, meas, bulk_b, extra_b, side_a, ints, sem):
    odd = lax.rem(where[0], 2)
    copies = []
    for side, flip in enumerate((odd, 1 - odd)):

        def place(at, count):
            if side == 1:
                return side_a.at[pl.ds(at, count)]
            return bulk_b.at[pl.ds(at, count)] if at < BULK else extra_b.at[pl.ds(at - BULK, count)]

        copies.append(
            pltpu.make_async_copy(labels.at[pl.ds(flip * (NP - HF), HF)], ints.at[side], sem.at[side, 8])
        )
        for l in range(4):
            copies.append(
                pltpu.make_async_copy(
                    start.at[l, pl.ds(flip * (NP - HF), HF)], place(l * HF, HF), sem.at[side, l]
                )
            )
            copies.append(
                pltpu.make_async_copy(
                    meas.at[l, pl.ds(flip * (NP - HM), HM)], place(4 * HF + l * HM, HM), sem.at[side, 4 + l]
                )
            )
    for copy in copies:
        copy.start()
    for copy in copies:
        copy.wait()
    extra_b[TOTAL - HF - BULK : TOTAL - BULK] = ints[0].astype(F32)
    side_a[TOTAL - HF : TOTAL] = ints[1].astype(F32)


def stages(where, spectra, absorb_t, half_t, lit, step, near, near2, state):
    fl, hd, wys, tmp, adj, ab, wes, wws, wzs, inv, ms = state
    gz = where[0]
    pad = jnp.zeros((PAD, N), F32)

    def inside(e):
        z = gz * NP + e - HF
        return jnp.where((z >= 0) & (z < 32 * NP), 1.0, 0.0).astype(F32)

    def clear(e, _):
        for l in range(4):
            for field in (fl, tmp, adj, hd):
                field[l, e, 0:PAD] = pad
                field[l, e, PAD + N : 2 * PAD + N] = pad
        return 0

    def optics(classes, e, r):
        there = inside(e)
        flat = pl.ds(r, CHUNK)
        rows = pl.ds(PAD + r, CHUNK)
        for l in range(4):
            ab[l, e, flat] = pick(classes, [absorb_t[l, i] for i in range(8)])
            hd[l, e, rows] = pick(classes, [half_t[l, i] * there for i in range(8)])

    def per_plane(ranges, fields, body):
        def spread(to, field, l):
            parts = [field[l, a:b, PAD : PAD + N].reshape((b - a) * N, N) for a, b in ranges]
            rows = parts[0] if len(parts) == 1 else jnp.concatenate(parts)
            both = jnp.dot(two_terms(rows), step[...], preferred_element_type=F32)
            at = 0
            for a, b in ranges:
                to[a:b] = both[at : at + (b - a) * N].reshape(b - a, N, 2 * N)
                at += (b - a) * N

        def outerloop(l, _):
            for to, field in zip((near, near2), fields):
                spread(to, field, l)

            def innerloop(e, _):
                for c in range(N // CHUNK):
                    body(l, e, c * CHUNK)
                return 0

            for a, b in ranges:
                lax.fori_loop(a, b, innerloop, 0)
            return 0

        lax.fori_loop(0, 4, outerloop, 0)

    def face(e):
        for l in range(4):
            for c in range(N // CHUNK):
                here = pl.ds(PAD + c * CHUNK, CHUNK)
                wzs[l, e, pl.ds(c * CHUNK, CHUNK)] = hd[l, e, here] + hd[l, e + 1, here]

    def moved(field, l, e, r):
        flat = pl.ds(r, CHUNK)
        here = pl.ds(PAD + r, CHUNK)
        north = pl.ds(PAD + r + 1, CHUNK)
        south = pl.ds(PAD + r - 1, CHUNK)
        return (
            wzs[l, e, flat] * field[l, e + 1, here]
            + wzs[l, e - 1, flat] * field[l, e - 1, here]
            + wys[l, e, here] * field[l, e, north]
            + wys[l, e, south] * field[l, e, south]
            + wes[l, e, flat] * near[e, flat, 0:N]
            + wws[l, e, flat] * near[e, flat, N : 2 * N]
        )

    def first(l, e, r):
        flat = pl.ds(r, CHUNK)
        here = pl.ds(PAD + r, CHUNK)
        north_rows = pl.ds(PAD + r + 1, CHUNK)
        south_rows = pl.ds(PAD + r - 1, CHUNK)
        h = hd[l, e, here]
        north = h + hd[l, e, north_rows]
        south = h + hd[l, e, south_rows]
        above = h + hd[l, e + 1, here]
        below = wzs[l, e - 1, flat]
        east = h + near2[e, flat, 0:N]
        west = h + near2[e, flat, N : 2 * N]
        if r == 0:
            wys[l, e, 0:PAD] = jnp.broadcast_to(h[0:1], (PAD, N))
        wys[l, e, here] = north
        wzs[l, e, flat] = above
        wes[l, e, flat] = east
        wws[l, e, flat] = west
        total = ab[l, e, flat] + above + below + north + south + east + west
        scale = inside(e) / total
        inv[l, e, flat] = scale
        flow = (
            above * fl[l, e + 1, here]
            + below * fl[l, e - 1, here]
            + north * fl[l, e, north_rows]
            + south * fl[l, e, south_rows]
            + east * near[e, flat, 0:N]
            + west * near[e, flat, N : 2 * N]
        )
        tmp[l, e, here] = (spectra[l, 5] * lit[flat] + flow) * scale

    def second(l, e, r):
        flat = pl.ds(r, CHUNK)
        here = pl.ds(PAD + r, CHUNK)
        scale = inv[l, e, flat]
        f = (spectra[l, 5] * lit[flat] + moved(tmp, l, e, r)) * scale
        fl[l, e, here] = f
        absorb = ab[l, e, flat]
        misfit = absorb * f - ms[l, e - (HF - HM), flat]
        ms[l, e - (HF - HM), flat] = misfit
        adj[l, e, here] = absorb * misfit * scale

    def third(l, e, r):
        flat = pl.ds(r, CHUNK)
        here = pl.ds(PAD + r, CHUNK)
        tmp[l, e, here] = (ab[l, e, flat] * ms[l, e - (HF - HM), flat] + moved(adj, l, e, r)) * inv[l, e, flat]

    def couple(l, e, r):
        flat = pl.ds(r, CHUNK)
        here = pl.ds(PAD + r, CHUNK)
        north = pl.ds(PAD + r + 1, CHUNK)
        south = pl.ds(PAD + r - 1, CHUNK)
        h = hd[l, e, here]
        f = fl[l, e, here]
        a = tmp[l, e, here]
        total = (
            wes[l, e, flat] * (near[e, flat, 0:N] - f) * (near2[e, flat, 0:N] - a)
            + wws[l, e, flat] * (near[e, flat, N : 2 * N] - f) * (near2[e, flat, N : 2 * N] - a)
            + wys[l, e, here] * (fl[l, e, north] - f) * (tmp[l, e, north] - a)
            + wys[l, e, south] * (fl[l, e, south] - f) * (tmp[l, e, south] - a)
            + wzs[l, e, flat] * (fl[l, e + 1, here] - f) * (tmp[l, e + 1, here] - a)
            + wzs[l, e - 1, flat] * (fl[l, e - 1, here] - f) * (tmp[l, e - 1, here] - a)
        )
        ab[l, e, flat] = 12.0 * h * h * total

    return inside, clear, optics, per_plane, face, first, second, third, couple


def inner_kernel(where, spectra, absorb_t, half_t, labels, illum, start, meas, *rest):
    state, (own, lit, step, near, near2, sem) = rest[:11], rest[11:]
    fl, hd, wys, tmp, adj, ab, wes, wws, wzs, inv, ms = state
    _, clear, optics, per_plane, face, first, second, third, _ = stages(
        where, spectra, absorb_t, half_t, lit, step, near, near2, state
    )
    copies = [
        pltpu.make_async_copy(labels, own, sem.at[0]),
        pltpu.make_async_copy(start, fl.at[:, pl.ds(HF, NP), pl.ds(PAD, N)], sem.at[1]),
        pltpu.make_async_copy(meas, ms.at[:, pl.ds(HM, NP)], sem.at[2]),
    ]
    for copy in copies:
        copy.start()
    lit[...] = illum[...].astype(F32)
    step[...] = shifts()
    lax.fori_loop(0, EXT, clear, 0)

    def optics_own(p, _):
        for c in range(N // CHUNK):
            optics(own[p, pl.ds(c * CHUNK, CHUNK)], p + HF, c * CHUNK)
        return 0

    copies[0].wait()
    lax.fori_loop(0, NP, optics_own, 0)
    face(HF)
    copies[1].wait()
    per_plane(((HF + 1, HF + NP - 1),), (fl, hd), first)
    copies[2].wait()
    per_plane(((HF + 2, HF + NP - 2),), (tmp,), second)
    per_plane(((HF + 3, HF + NP - 3),), (adj,), third)


def solve_kernel(
    where, spectra, absorb_t, half_t, illum, side_a, bulk_b, straight_b, turned_b, *rest,
):
    fluence, coef_a, coef_b, edge_a, edge_b, *rest = rest[11:]
    outs, state = rest[:6], rest[6:17]
    shared, lit, step, near, near2, sem = rest[17:]
    fl, hd, wys, tmp, adj, ab, wes, wws, wzs, inv, ms = state
    sends, keeps = outs[0::2], outs[1::2]
    inside, _, optics, per_plane, face, first, second, third, couple = stages(
        where, spectra, absorb_t, half_t, lit, step, near, near2, state
    )
    gz = where[0]
    me = where[1]
    odd = lax.rem(gz, 2)
    whole = pl.ds(PAD, N)

    def incoming(bulk, extra, high, number):
        def piece(at, count):
            return bulk.at[pl.ds(at, count)] if at < BULK else extra.at[pl.ds(at - BULK, count)]

        first = 3 + 9 * number
        lights = [
            pltpu.make_async_copy(
                piece(l * HF, HF), fl.at[l, pl.ds(high * (HF + NP), HF), whole], sem.at[first + l]
            )
            for l in range(4)
        ]
        pressures = [
            pltpu.make_async_copy(
                piece(4 * HF + l * HM, HM), ms.at[l, pl.ds(high * (HM + NP), HM)], sem.at[first + 4 + l]
            )
            for l in range(4)
        ]
        classes = pltpu.make_async_copy(
            piece(TOTAL - HF, HF), shared.at[pl.ds(high * HF, HF)], sem.at[first + 8]
        )
        return lights, pressures, classes

    rest_a = side_a.at[pl.ds(BULK, TOTAL - BULK)]
    lights_a, pressures_a, classes_a = incoming(side_a, rest_a, 1 - odd, 0)
    lights_b, pressures_b, classes_b = incoming(bulk_b, straight_b, odd, 1)
    _, turned_pressures, turned_classes = incoming(bulk_b, turned_b, odd, 1)
    label_copies = [classes_a, classes_b]
    meas_copies = pressures_a + pressures_b
    fluence_copies = lights_a + lights_b
    turned = (lax.rem(gz, 8) == 0) | (lax.rem(gz, 8) == 7)
    classes_a.start()

    @pl.when(turned)
    def _():
        turned_classes.start()
        for copy in turned_pressures[2:]:
            copy.start()

    @pl.when(jnp.logical_not(turned))
    def _():
        classes_b.start()
        for copy in pressures_b[2:]:
            copy.start()

    for copy in fluence_copies + pressures_a + pressures_b[:2]:
        copy.start()

    lit[...] = illum[...].astype(F32)
    step[...] = shifts()

    def optics_shared(p, _):
        e = p + jnp.where(p < HF, 0, NP)
        for c in range(N // CHUNK):
            classes = shared[p, pl.ds(c * CHUNK, CHUNK)].astype(jnp.int32)
            optics(classes, e, c * CHUNK)
        return 0

    for copy in label_copies:
        copy.wait()
    lax.fori_loop(0, 2 * HF, optics_shared, 0)
    for copy in fluence_copies:
        copy.wait()

    @pl.when(gz == 0)
    def _():
        fl[:, HF - 1] = jnp.zeros((4, N + 2 * PAD, N), F32)

    @pl.when(gz == 31)
    def _():
        fl[:, HF + NP] = jnp.zeros((4, N + 2 * PAD, N), F32)

    face(0)
    last = HF + NP
    per_plane(((1, HF + 1), (last - 1, EXT - 1)), (fl, hd), first)
    for copy in meas_copies:
        copy.wait()
    per_plane(((2, HF + 2), (last - 2, EXT - 2)), (tmp,), second)
    write = pltpu.make_async_copy(fl.at[:, pl.ds(HF, NP), whole], fluence, sem.at[0])
    write.start()
    for l in range(4):
        tmp[l, HF - 1] = jnp.zeros((N + 2 * PAD, N), F32)
        tmp[l, last] = jnp.zeros((N + 2 * PAD, N), F32)
    per_plane(((HF, HF + 3), (last - 3, last)), (adj,), third)
    per_plane(((HF, last),), (fl, tmp), couple)

    for coef, edge, high in ((coef_a, edge_a, 1 - odd), (coef_b, edge_b, odd)):
        e = HF + high * (NP - 1)
        beyond = e + 2 * high - 1
        face = e + high - 1
        for l in range(4):
            for c in range(N // CHUNK):
                here = pl.ds(PAD + c * CHUNK, CHUNK)
                to = pl.ds(c * CHUNK, CHUNK)
                h = hd[l, e, here]
                edge[l, to] = tmp[l, e, here]
                coef[l, to] = (
                    spectra[l, 4] * 12.0 * h * h * wzs[l, face, to] * (fl[l, beyond, here] - fl[l, e, here])
                )

    for code in range(8):
        rows = pl.ds(pl.multiple_of(PAD + (me ^ code) * ROWS, 8), ROWS)
        flat = pl.ds(pl.multiple_of((me ^ code) * ROWS, 8), ROWS)
        for plane in range(NP):
            e = plane + HF
            common = [fl[l, e, rows] * (ms[l, e - (HF - HM), flat] - tmp[l, e, rows]) for l in range(4)]
            paired = [ab[l, e, flat] for l in range(4)]
            for field in range(5):
                terms = common if field < 4 else paired
                value = spectra[0, field] * terms[0]
                for l in range(1, 4):
                    value = value + spectra[l, field] * terms[l]
                part, index = part_of(plane, field)
                slot = slot_of(part, code)
                if slot >= 4:
                    sends[part][slot - 4, index] = value
                else:
                    keeps[part][slot, index] = value
    write.wait()


def edge_kernel(where, coef_a, coef_b, edge_a, edge_b, send, keep):
    gz, me = where[0], where[1]
    there = jnp.where((gz > 0) & (gz < 31), 1.0, 0.0).astype(F32)
    for code in range(8):
        rows = pl.ds(pl.multiple_of((me ^ code) * ROWS, ROWS), ROWS)
        slot = slot_of(0, code)
        for side, (coef, edge) in enumerate(((coef_a, edge_a), (coef_b, edge_b))):
            value = coef[0, rows] * edge[0, rows]
            for l in range(1, 4):
                value = value + coef[l, rows] * edge[l, rows]
            if side:
                value = value * there
            if slot >= 4:
                send[slot - 4, side] = value
            else:
                keep[slot, side] = value


def squares_kernel(where, late_keep, late_recv, *refs):
    keeps, recvs, owns, sums = refs[:3], refs[3:6], refs[6:9], refs[9]
    odd = lax.rem(where[0], 2)
    total = [jnp.zeros((8, N), F32) for _ in range(5)]
    for plane in range(NP):
        for field in range(5):
            part, index = part_of(plane, field)
            value = keeps[part][0, index] + recvs[part][0, index]
            if field == 4 and plane in (0, NP - 1):
                side = 1 - odd if plane == 0 else odd
                value = value + (late_keep[0, side] + late_recv[0, side])
            owns[part][0, index] = value
            squared = value * value
            total[field] = total[field] + squared[:8] + squared[8:]
    lane = lax.broadcasted_iota(jnp.int32, (1, N), 1)
    row = jnp.zeros((1, N), F32)
    for field in range(5):
        whole = jnp.sum(jnp.sum(total[field], axis=0, keepdims=True), axis=1, keepdims=True)
        row = jnp.where(lane == field, whole, row)
    for target in range(32):
        sums[target] = row


def final_kernel(where, table, labels, *refs):
    pieces, (conc, scat, done, sem) = refs[:12], refs[12:]
    me = where[1]
    cells = 32 * NP * N * N
    extra = PARTS[0][1]
    total = pieces[0][0, extra] + pieces[1][0, extra]
    for i in range(2):
        total = total + pieces[2][i, extra]
    for i in range(4):
        total = total + pieces[3][i, extra]
    factor = -STEP / jnp.sqrt(total / cells + 1e-06)
    factors = [jnp.broadcast_to(factor[:, c : c + 1], (ROWS, N)) for c in range(5)]
    copies = []
    for plane in range(NP):
        for code in range(8):
            rows = pl.ds(pl.multiple_of((me ^ code) * ROWS, ROWS), ROWS)
            classes = labels[plane, rows]
            for field in range(5):
                part, index = part_of(plane, field)
                slot = slot_of(part, code)
                own, one, two, four = pieces[4 * part : 4 * part + 4]
                if slot == 0:
                    grad = own[0, index]
                elif slot == 1:
                    grad = one[0, index]
                elif slot < 4:
                    grad = two[slot - 2, index]
                else:
                    grad = four[slot - 4, index]
                coeff = pick(classes, [table[i, field] for i in range(8)])
                done[field, plane, rows] = coeff * jnp.exp(grad * factors[field])
        copies.append(pltpu.make_async_copy(done.at[0:4, plane], conc.at[:, plane], sem.at[plane, 0]))
        copies.append(pltpu.make_async_copy(done.at[4, plane], scat.at[plane], sem.at[plane, 1]))
        copies[-2].start()
        copies[-1].start()
    for copy in copies:
        copy.wait()


VMEM = pl.BlockSpec(memory_space=pltpu.VMEM)
SMEM = pl.BlockSpec(memory_space=pltpu.SMEM)
ANY = pl.BlockSpec(memory_space=pl.ANY)


def swap(x, code):
    return lax.ppermute(x, "wl", [(i, i ^ code) for i in range(8)])


ON_CHIP = [(i, i ^ 1) for i in range(32)]
OFF_CHIP = [(i, (i + 1 if i % 2 else i - 1) % 32) for i in range(32)]
AROUND = [(i, i - 7 if i % 8 == 7 else i + 7 if i % 8 == 0 else j) for i, j in OFF_CHIP]
ALONG = [(i, i + 8) for i in (0, 8, 16)] + [(i, i - 8) for i in (15, 23, 31)]


def beside(a, b):
    return lax.ppermute(a, "gz", ON_CHIP), lax.ppermute(b, "gz", OFF_CHIP)


def shards(labels, label_table, spectra, illumination, fluence_start, measured):
    where = jnp.stack([lax.axis_index("gz"), lax.axis_index("wl")]).astype(jnp.int32)
    small = pltpu.CompilerParams(vmem_limit_bytes=12 * 2**20)

    def in_hbm(x):
        return pltpu.with_memory_space_constraint(x, pltpu.HBM)

    def in_vmem(x):
        return pltpu.with_memory_space_constraint(x, pltpu.VMEM)

    bulk_b, extra_b, side_a = pl.pallas_call(
        pack_kernel,
        out_shape=[pltpu.VMEM((count, N, N), F32) for count in (BULK, TOTAL - BULK, TOTAL)],
        in_specs=[SMEM] + [ANY] * 3,
        out_specs=[VMEM] * 3,
        scratch_shapes=[pltpu.VMEM((2, HF, N, N), jnp.int32), pltpu.SemaphoreType.DMA((2, 9))],
        compiler_params=small,
        name="pack",
    )(where, *map(in_hbm, (labels, fluence_start, measured)))
    bulk_b = lax.ppermute(bulk_b, "gz", OFF_CHIP)
    straight_b = lax.ppermute(extra_b, "gz", AROUND)
    side_a = lax.ppermute(side_a, "gz", ON_CHIP)
    turned_b = lax.ppermute(straight_b, "gz", ALONG)
    side_a, bulk_b, straight_b, turned_b = map(in_vmem, (side_a, bulk_b, straight_b, turned_b))

    absorb_t = spectra[:, 0, None] * label_table[None, :, 0]
    for c in range(1, 4):
        absorb_t = absorb_t + spectra[:, c, None] * label_table[None, :, c]
    half_t = 0.5 / (3.0 * (absorb_t + spectra[:, 4, None] * label_table[None, :, 4]))

    sizes = [last - first for first, last in PARTS]
    held = (
        [pltpu.VMEM((4, EXT, N + 2 * PAD, N), F32)] * 5
        + [pltpu.VMEM((4, EXT, N, N), F32)] * 5
        + [pltpu.VMEM((4, NP + 2 * HM, N, N), F32)]
    )
    work = [
        pltpu.VMEM((N, N), F32),
        pltpu.VMEM((2 * N, 2 * N), jnp.bfloat16),
        pltpu.VMEM((EXT, N, 2 * N), F32),
        pltpu.VMEM((EXT, N, 2 * N), F32),
    ]
    state = pl.pallas_call(
        inner_kernel,
        out_shape=held,
        in_specs=[SMEM] * 4 + [ANY] + [VMEM] + [ANY] * 2,
        out_specs=[VMEM] * 11,
        scratch_shapes=[pltpu.VMEM((NP, N, N), jnp.int32)] + work + [pltpu.SemaphoreType.DMA((3,))],
        compiler_params=small,
        name="inner",
    )(where, spectra, absorb_t, half_t, in_hbm(labels), illumination, *map(in_hbm, (fluence_start, measured)))
    fluence, coef_a, coef_b, edge_a, edge_b, *out = pl.pallas_call(
        solve_kernel,
        out_shape=[jax.ShapeDtypeStruct((4, NP, N, N), F32)]
        + [pltpu.VMEM((4, N, N), F32)] * 4
        + [pltpu.VMEM((4, size, ROWS, N), F32) for size in sizes for _ in range(2)]
        + held,
        in_specs=[SMEM] * 4 + [VMEM] + [ANY] * 4 + [VMEM] * 11,
        out_specs=[ANY] + [VMEM] * 21,
        input_output_aliases={9 + i: 11 + i for i in range(11)},
        scratch_shapes=[pltpu.VMEM((2 * HF, N, N), F32)] + work + [pltpu.SemaphoreType.DMA((21,))],
        compiler_params=small,
        name="solve",
    )(where, spectra, absorb_t, half_t, illumination, side_a, bulk_b, straight_b, turned_b, *map(in_vmem, state))
    out = out[:6]
    sends = list(out[0::2])
    keeps = list(out[1::2])

    far_a, far_b = beside(edge_a, edge_b)
    for phase in range(2):
        recvs = [swap(sends[q], GENS[ORDERS[q][phase]]) for q in range(3)]
        half = keeps[0].shape[0] // 2
        sends = [keeps[q][half:] + recvs[q][half:] for q in range(3)]
        keeps = [keeps[q][:half] + recvs[q][:half] for q in range(3)]
        if phase == 0:
            far_a, far_b = lax.optimization_barrier((far_a, far_b, *sends))[:2]
    recvs = [swap(sends[q], GENS[ORDERS[q][2]]) for q in range(3)]

    late_send, late_keep = pl.pallas_call(
        edge_kernel,
        out_shape=[jax.ShapeDtypeStruct((4, 2, ROWS, N), F32)] * 2,
        in_specs=[SMEM] + [VMEM] * 4,
        out_specs=[VMEM] * 2,
        compiler_params=small,
        name="edge",
    )(where, coef_a, coef_b, far_a, far_b)
    for phase in range(2):
        late_recv = swap(late_send, GENS[ORDERS[0][phase]])
        half = late_keep.shape[0] // 2
        late_send = late_keep[half:] + late_recv[half:]
        late_keep = late_keep[:half] + late_recv[:half]
    late_recv = swap(late_send, GENS[ORDERS[0][2]])

    *owns, sums = pl.pallas_call(
        squares_kernel,
        out_shape=[jax.ShapeDtypeStruct((1, size, ROWS, N), F32) for size in sizes]
        + [jax.ShapeDtypeStruct((32, 1, N), F32)],
        in_specs=[SMEM] + [VMEM] * 8,
        out_specs=[VMEM] * 4,
        compiler_params=small,
        name="squares",
    )(where, late_keep, late_recv, *keeps, *recvs)

    steps = {q: [owns[q]] for q in (1, 2)}
    for phase in (2, 1, 0):
        for q in (1, 2):
            have = steps[q]
            mine = have[0] if len(have) == 1 else jnp.concatenate(have)
            have.append(swap(mine, GENS[ORDERS[q][phase]]))
    slab = jnp.sum(lax.all_to_all(sums, "gz", 0, 0), axis=0)
    steps[0] = [jnp.concatenate([owns[0], jnp.broadcast_to(slab[None, None], (1, 1, ROWS, N))], axis=1)]
    for phase in (2, 1, 0):
        have = steps[0]
        mine = have[0] if len(have) == 1 else jnp.concatenate(have)
        have.append(swap(mine, GENS[ORDERS[0][phase]]))
    pieces = steps[0] + steps[1] + steps[2]
    conc, scat = pl.pallas_call(
        final_kernel,
        out_shape=[jax.ShapeDtypeStruct((4, NP, N, N), F32), jax.ShapeDtypeStruct((NP, N, N), F32)],
        in_specs=[SMEM] * 2 + [VMEM] * 13,
        out_specs=[ANY] * 2,
        scratch_shapes=[pltpu.VMEM((5, NP, N, N), F32), pltpu.SemaphoreType.DMA((NP, 2))],
        compiler_params=pltpu.CompilerParams(vmem_limit_bytes=32 * 2**20),
        name="final",
    )(where, label_table, labels, *pieces)
    return fluence, conc, scat


def solution(mesh):
    in_specs = (
        P("gz", None, None),
        P(),
        P("wl", None),
        P(),
        P("wl", "gz", None, None),
        P("wl", "gz", None, None),
    )
    out_specs = (P("wl", "gz", None, None), P(None, "gz", None, None), P("gz", None, None))
    return jax.shard_map(shards, mesh=mesh, in_specs=in_specs, out_specs=out_specs, check_vma=False)
```
